128 devices in a mesh: ctx: 16 (over x, y), tp: 8 (over z, core).
Axes of the slice: x: 4, y: 4, z: 4, core: 2. Of those that a mesh axis runs over, the one named last changes fastest.
Arguments:
- hidden_states: bfloat16 [32, 8192], P(None, 'ctx'), may hold values from -24 to 24
- norm_gain: bfloat16 [8192], P('ctx'), may hold values from 0.25 to 1.75
- prompt_lengths: int32 [8], replicated, may hold values from 1 to 16384, 73728 in all
- kv_cache: bfloat16 [8, 16384, 2, 1024], P(None, ('ctx', 'tp')), may hold values from -124 to 124
- w_qkv: bfloat16 [8192, 10240], P('ctx', 'tp'), may hold values from -0.0625 to 0.0625
- w_out: bfloat16 [8192, 8192], P('tp', 'ctx'), may hold values from -0.0625 to 0.0625
Outputs:
- block_out: bfloat16 [32, 8192], P(None, 'ctx')
- kv_decode: bfloat16 [16, 128, 64, 2, 1024], P('ctx', None, None, None, 'tp')
The draws below stay inside these ranges and needn't reach their ends.
Inputs may be any that keep to these rules, and one draw needn't show every extreme that they name: `prompt_lengths`: cache positions at or beyond a request's length are padding. Some request has exactly 16384.
All inputs are finite; a program needn't handle non-finite values.
Results may differ from the reference program's by a relative error of at most 0.012.
The reference program's roundings to bfloat16 on the way (of `scaled`, `query` and `attn`) count: a program that leaves them out, or rounds other values in their place, can miss the bound.
Values may be sent and summed in bfloat16 or wider, within the bound.
No kernel may reach another device: no remote copies, remote signals or barrier semaphores. Data moves between devices by JAX's collectives and lax.ppermute only.
A program may use at most 64 MiB of HBM per device.

```python
import math
import jax
import jax.numpy as jnp
import numpy as np
from jax import lax

D = 8192
H = 64
KVH = 8
HD = 128
REQUESTS = 8
STEPS = 4
SEQ = 16384
GQA = 8
ROWS = 32
SPLIT = 2
SOURCES = 128
PIECE = 64


def draw_hidden_states(key, part):
    key = jax.random.fold_in(key, 11)
    column = jnp.arange(D, dtype=jnp.float32) / D
    base = jax.random.truncated_normal(key, -6.0, 6.0, (ROWS, D), jnp.float32)
    values = base * jnp.sqrt(1.0 + 2.0 * column)
    return values.astype(jnp.bfloat16)


def draw_kv_cache(key, part):
    key = jax.random.fold_in(key, 23)
    first = jax.random.fold_in(key, 0)
    is_key = (jnp.arange(2, dtype=jnp.int32) == 0)[None, None, :, None]
    base = jax.random.truncated_normal(first, -4.0, 4.0, (REQUESTS, SEQ, 2, KVH * HD), jnp.float32)
    base = base * jnp.where(is_key, 2.6, 2.0)
    return base.astype(jnp.bfloat16)


def shard_levels(own_key, shape, shards, least, top_value):
    factor_of = 1.0
    for dim, blocks in shards:
        steps = jax.random.uniform(jax.random.fold_in(jax.random.fold_in(own_key, 6), dim), (blocks,), jnp.float32, least / len(shards), top_value / len(shards))
        factor_of = factor_of * jnp.repeat(jnp.exp(steps), shape[dim] // blocks).reshape((-1,) + (1,) * (len(shape) - 1 - dim))
    return factor_of


def length_profile(count, total, reach, lean):
    loads = [(1 << 20) // math.isqrt(rank ** lean) + 1 for rank in range(2, count + 1)]
    rest, counts = total - reach - (count - 1), [1] * (count - 1)
    while rest > 0:
        free = [i for i in range(count - 1) if counts[i] < reach]
        pool, budget = sum([loads[i] for i in free]), rest
        for i in free:
            more = min(reach - counts[i], max(1, budget * loads[i] // pool), rest)
            counts[i] = counts[i] + more
            rest = rest - more
    return np.array([reach] + counts)


def ragged_sizes(stream_key, number_of, total, reach, lean):
    if number_of == 2:
        one = jax.random.randint(stream_key, (), max(1, total - reach), min(reach, total - 1) + 1)
        return jnp.stack([one, total - one])
    sizes = jnp.asarray(length_profile(number_of, total, reach, lean), jnp.int32)
    pairs = (number_of - 1) // 2
    giver, sink = sizes[1:1 + 2 * pairs:2], sizes[2:2 + 2 * pairs:2]
    room = jnp.minimum(giver - 1, reach - sink)
    passed = jax.random.randint(jax.random.fold_in(stream_key, 1), (pairs,), 0, 1 << 20) % (room + 1)
    sizes = sizes.at[1:1 + 2 * pairs:2].set(giver - passed).at[2:2 + 2 * pairs:2].set(sink + passed)
    return sizes[jax.random.permutation(jax.random.fold_in(stream_key, 2), number_of)]


def normal_values(rng, shape, deviation, most, cuts=(), kind=jnp.bfloat16):
    factor_of = shard_levels(rng, shape, cuts, -0.22, 0.18) if cuts else 1.0
    entries = jax.random.normal(rng, shape, jnp.float32) * deviation * factor_of
    return jnp.minimum(jnp.maximum(entries, -most), most).astype(kind)


def setup_inputs(seed: int = 0) -> dict:
    arg_keys = jax.random.split(jax.random.key(seed), 7)
    hidden_states = draw_hidden_states(jax.random.fold_in(arg_keys[6], 71), 0)
    norm_gain = jnp.clip(1.0 + 0.15 * jax.random.normal(arg_keys[1], (D,), jnp.float32), 0.25, 1.75).astype(jnp.bfloat16)
    prompt_lengths = ragged_sizes(arg_keys[2], REQUESTS, REQUESTS * SEQ // 2 + SEQ // 2, SEQ, 2).astype(jnp.int32)
    kv_cache = draw_kv_cache(jax.random.fold_in(arg_keys[6], 71), 0)
    w_qkv = normal_values(arg_keys[4], (D, KVH * (GQA + 2) * HD), D ** -0.5, 0.0625, ((0, 16), (1, 8)))
    w_out = normal_values(arg_keys[5], (H * HD, D), (H * HD) ** -0.5, 0.0625, ((0, 8), (1, 16)))
    return dict(hidden_states=hidden_states, norm_gain=norm_gain, prompt_lengths=prompt_lengths, kv_cache=kv_cache, w_qkv=w_qkv, w_out=w_out)


ROPE_BASE = 500000.0
ROPE_FACTOR = 8.0
LOW_FACTOR = 1.0
HIGH_FACTOR = 4.0
ROPE_ANCHOR = 8192.0

def angles(positions, width):
    base_freq = ROPE_BASE ** (-(2.0 * jnp.arange(width // 2, dtype=jnp.float32)) / width)
    wavelength = 2.0 * math.pi / base_freq
    blend = (ROPE_ANCHOR / wavelength - LOW_FACTOR) / (HIGH_FACTOR - LOW_FACTOR)
    middle = (1.0 - blend) * base_freq / ROPE_FACTOR + blend * base_freq
    freq = jnp.where(wavelength > ROPE_ANCHOR / LOW_FACTOR, base_freq / ROPE_FACTOR, jnp.where(wavelength < ROPE_ANCHOR / HIGH_FACTOR, base_freq, middle))
    return positions.astype(jnp.float32)[..., None] * freq

def rotate(vec, angle):
    half = vec.shape[-1] // 2
    first = vec[..., :half]
    second = vec[..., half:]
    cosine = jnp.cos(angle)
    sine = jnp.sin(angle)
    return jnp.concatenate([first * cosine - second * sine, second * cosine + first * sine], axis=-1)

def reference(hidden_states, norm_gain, prompt_lengths, kv_cache, w_qkv, w_out):
    values_in = hidden_states.astype(jnp.float32)
    square = lax.optimization_barrier(jnp.sum(values_in * values_in, axis=1))
    scaled = (values_in * norm_gain.astype(jnp.float32)).astype(jnp.bfloat16)
    proj = jnp.dot(scaled, w_qkv, preferred_element_type=jnp.float32)
    proj = proj * lax.rsqrt(square / D + 1e-05)[:, None]
    proj = proj.reshape(STEPS, REQUESTS, KVH, GQA + 2, HD)
    step_index = jnp.arange(STEPS, dtype=jnp.int32)
    positions = prompt_lengths[None, :] + step_index[:, None]
    angle = angles(positions, HD)[:, :, None, None, :]
    query = rotate(proj[:, :, :, :GQA], angle).astype(jnp.bfloat16)
    key_new = rotate(proj[:, :, :, GQA], angle[:, :, :, 0]).astype(jnp.bfloat16)
    value_new = proj[:, :, :, GQA + 1].astype(jnp.bfloat16)
    scale = HD ** (-0.5)
    cache_pos = jnp.arange(SEQ, dtype=jnp.int32)
    causal = step_index[:, None] >= step_index[None, :]

    def one_request(index):
        length = prompt_lengths[index]
        cache = lax.dynamic_index_in_dim(kv_cache, index, 0, keepdims=False)
        keys = cache[:, 0].reshape(SEQ, KVH, HD).astype(jnp.float32)
        values = cache[:, 1].reshape(SEQ, KVH, HD).astype(jnp.float32)
        asked = lax.dynamic_index_in_dim(query, index, 1, keepdims=False).astype(jnp.float32)
        fresh_keys = lax.dynamic_index_in_dim(key_new, index, 1, keepdims=False).astype(jnp.float32)
        fresh_values = lax.dynamic_index_in_dim(value_new, index, 1, keepdims=False).astype(jnp.float32)
        old = jnp.einsum('tkgd,skd->kgts', asked, keys) * scale
        old = jnp.where(cache_pos < length, old, -1e+30)
        new = jnp.einsum('tkgd,ukd->kgtu', asked, fresh_keys) * scale
        new = jnp.where(causal, new, -1e+30)
        top = jnp.maximum(lax.optimization_barrier(jnp.max(old, axis=-1)), lax.optimization_barrier(jnp.max(new, axis=-1)))
        weight_old = jnp.exp(old - top[..., None])
        weight_new = jnp.exp(new - top[..., None])
        total = lax.optimization_barrier(jnp.sum(weight_old, axis=-1)) + lax.optimization_barrier(jnp.sum(weight_new, axis=-1))
        mixed = jnp.einsum('kgts,skd->tkgd', weight_old.astype(jnp.bfloat16).astype(jnp.float32), values)
        mixed = mixed + jnp.einsum('kgtu,ukd->tkgd', weight_new.astype(jnp.bfloat16).astype(jnp.float32), fresh_values)
        return mixed / jnp.transpose(total, (2, 0, 1))[..., None]
    attn = lax.map(one_request, jnp.arange(REQUESTS, dtype=jnp.int32))
    attn = jnp.transpose(attn, (1, 0, 2, 3, 4)).reshape(ROWS, H * HD).astype(jnp.bfloat16)
    block_out = jnp.dot(attn, w_out, preferred_element_type=jnp.float32).astype(jnp.bfloat16)
    cache_split = kv_cache.reshape(REQUESTS, SOURCES, SPLIT, PIECE, 2, KVH * HD)
    kv_decode = jnp.transpose(cache_split, (0, 2, 1, 3, 4, 5)).reshape(REQUESTS * SPLIT, SOURCES, PIECE, 2, KVH * HD)
    return (block_out, kv_decode)
```

```python
import math

import jax
import jax.numpy as jnp
from jax import lax
from jax.experimental import pallas as pl
from jax.experimental.pallas import tpu as pltpu
from jax.sharding import PartitionSpec as P

D = 8192
HD = 128
STEPS = 4
GQA = 8
REQUESTS = 8
SOURCES = 128
PIECE = 64
TP = 8
CTX = 16
HEAD_ROWS = STEPS * GQA

ROPE_BASE = 500000.0
ROPE_FACTOR = 8.0
LOW_FACTOR = 1.0
HIGH_FACTOR = 4.0
ROPE_ANCHOR = 8192.0
NEGATIVE = -1e30
SCALE = HD ** (-0.5)


def angles(positions, width):
    base_freq = ROPE_BASE ** (-(2.0 * jnp.arange(width // 2, dtype=jnp.float32)) / width)
    wavelength = 2.0 * math.pi / base_freq
    blend = (ROPE_ANCHOR / wavelength - LOW_FACTOR) / (HIGH_FACTOR - LOW_FACTOR)
    middle = (1.0 - blend) * base_freq / ROPE_FACTOR + blend * base_freq
    freq = jnp.where(
        wavelength > ROPE_ANCHOR / LOW_FACTOR,
        base_freq / ROPE_FACTOR,
        jnp.where(wavelength < ROPE_ANCHOR / HIGH_FACTOR, base_freq, middle),
    )
    return positions.astype(jnp.float32)[..., None] * freq


COLUMNS = (GQA + 2) * HD
SIDE = 4


def partial_kernel(x_ref, hidden_ref, gain_ref, w_ref, *out_refs):
    rows = STEPS * REQUESTS
    share = rows // SIDE
    target = lax.broadcasted_iota(jnp.int32, (rows, rows), 0)
    origin = lax.broadcasted_iota(jnp.int32, (rows, rows), 1)
    receiver = jnp.bitwise_xor(target // share, x_ref[0])
    request = receiver * (REQUESTS // SIDE) + target % share // STEPS
    moves = jnp.where(origin == target % STEPS * REQUESTS + request, 1.0, 0.0)
    values = jnp.dot(
        moves.astype(jnp.bfloat16), hidden_ref[...], preferred_element_type=jnp.float32
    )
    square = jnp.sum(values * values, axis=1, keepdims=True)
    gain = gain_ref[...].astype(jnp.float32).reshape(1, -1)
    scaled = (values * gain).astype(jnp.bfloat16)
    proj = jnp.dot(scaled, w_ref[...], preferred_element_type=jnp.float32)
    square = jnp.broadcast_to(square, (rows, HD))
    for index, out_ref in enumerate(out_refs):
        out_ref[:, pl.ds(0, COLUMNS)] = proj[index * share:(index + 1) * share]
        out_ref[:, pl.ds(COLUMNS, HD)] = square[index * share:(index + 1) * share]


def partial_projection(x, hidden_states, norm_gain, w_qkv):
    vmem = pl.BlockSpec(memory_space=pltpu.VMEM)
    shape = jax.ShapeDtypeStruct((STEPS * REQUESTS // SIDE, COLUMNS + HD), jnp.float32)
    return pl.pallas_call(
        partial_kernel,
        in_specs=[pl.BlockSpec(memory_space=pltpu.SMEM), vmem, vmem, vmem],
        out_specs=[vmem] * SIDE,
        out_shape=[shape] * SIDE,
        compiler_params=pltpu.CompilerParams(vmem_limit_bytes=8 * 1024 * 1024),
        name="partial_projection",
    )(x.reshape(1), hidden_states, norm_gain, w_qkv)


def swap(value, axis, other):
    pairs = [(index, index ^ other) for index in range(lax.axis_size(axis))]
    return lax.ppermute(value, axis, pairs)


def prep_kernel(kv_ref, out_ref, held, ready, in_sems, head_sems, out_sems):
    def fetch(receiver):
        return pltpu.make_async_copy(
            kv_ref.at[receiver], held.at[receiver // 2], in_sems.at[receiver // 2]
        )

    def fetch_head(receiver, head):
        return pltpu.make_async_copy(
            kv_ref.at[receiver, :, :, pl.ds(head * HD, HD)],
            ready.at[receiver, head],
            head_sems.at[receiver // 2, head],
        )

    def place(receiver):
        return pltpu.make_async_copy(
            ready.at[receiver], out_ref.at[receiver], out_sems.at[receiver]
        )

    for receiver in range(0, CTX, 2):
        fetch(receiver).start()
        for head in range(TP):
            fetch_head(receiver + 1, head).start()
    for receiver in range(0, CTX, 2):
        fetch(receiver).wait()
        for head in range(TP):
            ready[receiver, head] = held[receiver // 2, :, :, pl.ds(head * HD, HD)]
        place(receiver).start()
        for head in range(TP):
            fetch_head(receiver + 1, head).wait()
        place(receiver + 1).start()
    for receiver in range(CTX):
        place(receiver).wait()


def prep(kv_cache):
    split = kv_cache.reshape(CTX, PIECE, 2, TP * HD)
    return pl.pallas_call(
        prep_kernel,
        out_shape=jax.ShapeDtypeStruct((CTX, TP, PIECE, 2, HD), jnp.bfloat16),
        in_specs=[pl.BlockSpec(memory_space=pl.ANY)],
        out_specs=pl.BlockSpec(memory_space=pl.ANY),
        scratch_shapes=[
            pltpu.VMEM((CTX // 2, PIECE, 2, TP * HD), jnp.bfloat16),
            pltpu.VMEM((CTX, TP, PIECE, 2, HD), jnp.bfloat16),
            pltpu.SemaphoreType.DMA((CTX // 2,)),
            pltpu.SemaphoreType.DMA((CTX // 2, TP)),
            pltpu.SemaphoreType.DMA((CTX,)),
        ],
        compiler_params=pltpu.CompilerParams(vmem_limit_bytes=56 * 1024 * 1024),
        cost_estimate=pl.CostEstimate(
            flops=0, transcendentals=0, bytes_accessed=4 * kv_cache.size
        ),
        name="cache_by_receiver",
    )(split)


CHUNKS = 4
CHUNK_CTX = CTX // CHUNKS
CHUNK_SOURCES = SOURCES // CHUNKS
CHUNK_KEYS = CHUNK_SOURCES * PIECE
CHUNK_ROWS = CHUNK_KEYS * 2
STATE_ROWS = HEAD_ROWS + 16


def attend_kernel(
    info_ref, kv_ref, own_ref, first_ref, second_ref, third_ref, cos_ref, sin_ref,
    kv_out_ref, out_ref,
    held, wide, pairs, query, scores, peaks, top, total, acc, in_sems, out_sems,
):
    length = info_ref[0]
    part = info_ref[1]
    left = length - part * PIECE

    def fetch(ctx):
        return pltpu.make_async_copy(kv_ref.at[ctx], held.at[ctx], in_sems.at[ctx])

    def place(ctx):
        return pltpu.make_async_copy(held.at[ctx], kv_out_ref.at[ctx], out_sems.at[ctx])

    for ctx in range(CTX):
        fetch(ctx).start()

    row = lax.broadcasted_iota(jnp.int32, (HEAD_ROWS, HD), 0)
    lane = lax.broadcasted_iota(jnp.int32, (HEAD_ROWS, HD), 1)
    slot = lane // PIECE * (2 * PIECE) + lane % PIECE

    summed = own_ref[...] + first_ref[...] + second_ref[...] + third_ref[...]
    norm = lax.rsqrt(summed[:, COLUMNS:] / D + 1e-05)

    def head(index):
        return summed[:, index * HD:(index + 1) * HD] * norm

    def turn(vec):
        return vec * cos_ref[...] + pltpu.roll(vec, HD // 2, 1) * sin_ref[...]

    query[...] = jnp.concatenate([turn(head(g)) for g in range(GQA)], axis=0).astype(jnp.bfloat16)
    rest = jnp.zeros((HD - STEPS, HD), jnp.float32)
    keys = jnp.concatenate([turn(head(GQA)), rest], axis=0).astype(jnp.bfloat16)
    values = jnp.concatenate([head(GQA + 1), rest], axis=0).astype(jnp.bfloat16)
    fresh = lax.dot_general(
        query[...], keys, (((1,), (1,)), ((), ())), preferred_element_type=jnp.float32
    ) * SCALE
    live = jnp.logical_and(lane <= row % STEPS, part == 0)
    fresh = jnp.where(live, fresh, NEGATIVE)
    high = jnp.max(fresh, axis=1, keepdims=True)
    weight = jnp.where(live, jnp.exp(fresh - high), 0.0)
    top[...] = jnp.broadcast_to(high, (HEAD_ROWS, HD))
    total[...] = weight
    acc[...] = jnp.dot(weight.astype(jnp.bfloat16), values, preferred_element_type=jnp.float32)

    def arrive(chunk):
        for ctx in range(chunk * CHUNK_CTX, (chunk + 1) * CHUNK_CTX):
            fetch(ctx).wait()
            place(ctx).start()

    def score(chunk):
        wide[...] = held[pl.ds(chunk * CHUNK_CTX, CHUNK_CTX)].reshape(CHUNK_ROWS, HD).astype(
            jnp.float32
        )
        for index in range(2):
            pairs[chunk % 2, index] = wide[pl.ds(index, CHUNK_KEYS, stride=2), :].astype(
                jnp.bfloat16
            )
        found = lax.dot_general(
            query[...],
            pairs[chunk % 2, 0],
            (((1,), (1,)), ((), ())),
            preferred_element_type=jnp.float32,
        )
        peak = None
        for index in range(CHUNK_KEYS // HD):
            source = chunk * CHUNK_SOURCES + index * 2
            piece = found[:, index * HD:(index + 1) * HD] * SCALE
            piece = jnp.where(slot < left - source * (2 * PIECE), piece, NEGATIVE)
            scores[chunk % 2, :, pl.ds(index * HD, HD)] = piece
            peak = piece if peak is None else jnp.maximum(peak, piece)
        peaks[chunk % 2] = peak

    def fold(chunk):
        high = jnp.maximum(top[...], jnp.max(peaks[chunk % 2], axis=1, keepdims=True))
        fade = jnp.exp(top[...] - high)
        summed = total[...] * fade
        pieces = []
        for index in range(CHUNK_KEYS // HD):
            weight = jnp.exp(scores[chunk % 2, :, pl.ds(index * HD, HD)] - high)
            summed = summed + weight
            pieces.append(weight.astype(jnp.bfloat16))
        top[...] = high
        total[...] = summed
        acc[...] = acc[...] * fade + jnp.dot(
            jnp.concatenate(pieces, axis=1),
            pairs[chunk % 2, 1],
            preferred_element_type=jnp.float32,
        )

    arrive(0)

    @pl.when(left > 0)
    def _():
        score(0)

    for chunk in range(CHUNKS):
        if chunk + 1 < CHUNKS:
            arrive(chunk + 1)

        @pl.when(chunk * CHUNK_SOURCES * 2 * PIECE < left)
        def _(chunk=chunk):
            if chunk + 1 < CHUNKS:
                score(chunk + 1)
            fold(chunk)

    count = jnp.sum(total[...], axis=1, keepdims=True)
    some = count > 0.0
    safe = jnp.where(some, count, 1.0)
    out_ref[pl.ds(0, HEAD_ROWS), :] = (acc[...] / safe).astype(jnp.bfloat16)
    level = jnp.where(some, top[...] + jnp.log(safe), NEGATIVE)
    level = jnp.sum(jnp.where(row == lane, level, 0.0), axis=0, keepdims=True)
    first = level.astype(jnp.bfloat16).astype(jnp.float32)
    second = (level - first).astype(jnp.bfloat16).astype(jnp.float32)
    third = level - first - second
    place_in = lax.broadcasted_iota(jnp.int32, (16, HD), 0)
    parts = jnp.where(place_in == 0, first, jnp.where(place_in == 1, second, third))
    out_ref[pl.ds(HEAD_ROWS, 16), :] = parts.astype(jnp.bfloat16)

    for ctx in range(CTX):
        place(ctx).wait()


def attend(info, moved, sums, cosine, sine):
    anywhere = pl.BlockSpec(memory_space=pl.ANY)
    vmem = pl.BlockSpec(memory_space=pltpu.VMEM)
    return pl.pallas_call(
        attend_kernel,
        in_specs=[pl.BlockSpec(memory_space=pltpu.SMEM), anywhere] + [vmem] * 6,
        out_specs=[anywhere, vmem],
        scratch_shapes=[
            pltpu.VMEM((CTX, TP, 2 * PIECE, HD), jnp.bfloat16),
            pltpu.VMEM((CHUNK_ROWS, HD), jnp.float32),
            pltpu.VMEM((2, 2, CHUNK_KEYS, HD), jnp.bfloat16),
            pltpu.VMEM((HEAD_ROWS, HD), jnp.bfloat16),
            pltpu.VMEM((2, HEAD_ROWS, CHUNK_KEYS), jnp.float32),
            pltpu.VMEM((2, HEAD_ROWS, HD), jnp.float32),
            pltpu.VMEM((HEAD_ROWS, HD), jnp.float32),
            pltpu.VMEM((HEAD_ROWS, HD), jnp.float32),
            pltpu.VMEM((HEAD_ROWS, HD), jnp.float32),
            pltpu.SemaphoreType.DMA((CTX,)),
            pltpu.SemaphoreType.DMA((CTX,)),
        ],
        out_shape=[
            jax.ShapeDtypeStruct((CTX, TP, 2 * PIECE, HD), jnp.bfloat16),
            jax.ShapeDtypeStruct((STATE_ROWS, HD), jnp.bfloat16),
        ],
        compiler_params=pltpu.CompilerParams(vmem_limit_bytes=24 * 1024 * 1024),
        name="attend",
    )(info, moved, *sums, cosine, sine)


def project_kernel(own_states_ref, mate_states_ref, own_ref, mate_ref, out_ref):
    row = lax.broadcasted_iota(jnp.int32, (HEAD_ROWS, HD), 0)
    lane = lax.broadcasted_iota(jnp.int32, (HEAD_ROWS, HD), 1)
    many = REQUESTS * HEAD_ROWS
    target = lax.broadcasted_iota(jnp.int32, (many, many), 0)
    origin = lax.broadcasted_iota(jnp.int32, (many, many), 1)
    head = target // (STEPS * REQUESTS)
    step = target // REQUESTS % STEPS
    request = target % REQUESTS
    moves = jnp.where(origin == request * HEAD_ROWS + head * STEPS + step, 1.0, 0.0)
    moves = moves.astype(jnp.bfloat16)
    totals = []
    for states_ref, w_ref in ((own_states_ref, own_ref), (mate_states_ref, mate_ref)):
        rows = []
        for request in range(REQUESTS):
            spots = [2 * request + part for part in range(2)]
            levels = []
            for spot in spots:
                coded = states_ref[spot, pl.ds(HEAD_ROWS, 16), :].astype(jnp.float32)
                level = coded[0:1] + coded[1:2] + coded[2:3]
                levels.append(jnp.sum(jnp.where(row == lane, level, 0.0), axis=1, keepdims=True))
            high = jnp.maximum(levels[0], levels[1])
            shares = [jnp.exp(level - high) for level in levels]
            whole = shares[0] + shares[1]
            mixed = sum(
                states_ref[spot, pl.ds(0, HEAD_ROWS), :].astype(jnp.float32) * (share / whole)
                for spot, share in zip(spots, shares)
            )
            rows.append(mixed.astype(jnp.bfloat16))
        attn = jnp.dot(
            moves, jnp.concatenate(rows, axis=0), preferred_element_type=jnp.float32
        ).astype(jnp.bfloat16)
        total = jnp.zeros(out_ref.shape, jnp.float32)
        for index in range(GQA):
            total = total + jnp.dot(
                attn[index * HEAD_ROWS:(index + 1) * HEAD_ROWS],
                w_ref[pl.ds(index * HD, HD), :],
                preferred_element_type=jnp.float32,
            )
        totals.append(total)
    out_ref[...] = (totals[0] + totals[1]).astype(jnp.bfloat16)


def project(states, mate_states, w_own, w_mate):
    vmem = pl.BlockSpec(memory_space=pltpu.VMEM)
    return pl.pallas_call(
        project_kernel,
        in_specs=[vmem] * 4,
        out_specs=vmem,
        out_shape=jax.ShapeDtypeStruct((STEPS * REQUESTS, w_own.shape[1]), jnp.bfloat16),
        compiler_params=pltpu.CompilerParams(vmem_limit_bytes=8 * 1024 * 1024),
        name="project",
    )(states, mate_states, w_own, w_mate)


def per_device(hidden_states, norm_gain, prompt_lengths, kv_cache, w_qkv, w_out):
    x = lax.axis_index("x")
    y = lax.axis_index("y")
    mine = x * (REQUESTS // SIDE) + y // 2
    part = y % 2
    length = lax.dynamic_index_in_dim(prompt_lengths, mine, 0, keepdims=False)

    ready = prep(kv_cache).reshape(CTX * TP, 2 * PIECE, HD)
    everyone = ("x", "y", "z", "core")
    moved = lax.all_to_all(ready, everyone, split_axis=0, concat_axis=0, tiled=True)
    moved = moved.reshape(CTX, TP, 2 * PIECE, HD)

    _, hidden_states = lax.optimization_barrier((ready, hidden_states))
    packed = partial_projection(x, hidden_states, norm_gain, w_qkv)
    packed, w_out = lax.optimization_barrier((packed, w_out))
    along_x = packed[0] + sum(swap(packed[k], "x", k) for k in range(1, SIDE))
    w_mate = swap(w_out, "core", 1)
    along_x = along_x.reshape(2, STEPS, COLUMNS + HD)
    own = lax.dynamic_index_in_dim(along_x, y // 2, 0, keepdims=False)
    far = lax.dynamic_index_in_dim(along_x, 1 - y // 2, 0, keepdims=False)
    sums = [own, swap(own, "y", 1), swap(far, "y", 2), swap(far, "y", 3)]

    angle = angles(length + jnp.arange(STEPS, dtype=jnp.int32), HD)
    cosine = jnp.cos(angle)
    sine = jnp.sin(angle)
    cosine = jnp.concatenate([cosine, cosine], axis=1)
    sine = jnp.concatenate([-sine, sine], axis=1)
    info = jnp.stack([length, part]).astype(jnp.int32)
    kv_decode, state = attend(info, moved, sums, cosine, sine)
    kv_decode = kv_decode.reshape(1, SOURCES, PIECE, 2, HD)

    states = jnp.broadcast_to(state[None], (CTX, STATE_ROWS, HD))
    states = lax.all_to_all(states, ("x", "y"), split_axis=0, concat_axis=0, tiled=True)
    out = project(states, swap(states, "core", 1), w_out, w_mate)
    terms = [out] + [swap(out, "z", other) for other in range(1, SIDE)]
    terms = [term.astype(jnp.float32) for term in terms]
    block_out = ((terms[0] + terms[1]) + (terms[2] + terms[3])).astype(jnp.bfloat16)
    return (block_out, kv_decode)


def solution(mesh):
    fine = jax.sharding.Mesh(
        mesh.devices.reshape(SIDE, SIDE, SIDE, 2), ("x", "y", "z", "core")
    )
    ctx, tp = ("x", "y"), ("z", "core")
    return jax.shard_map(
        per_device,
        mesh=fine,
        in_specs=(
            P(None, ctx),
            P(ctx),
            P(),
            P(None, ctx + tp, None, None),
            P(ctx, tp),
            P(tp, ctx),
        ),
        out_specs=(P(None, ctx), P(ctx, None, None, None, tp)),
        check_vma=False,
    )
```

```python
import math

import jax
import jax.numpy as jnp
from jax import lax
from jax.experimental import pallas as pl
from jax.experimental.pallas import tpu as pltpu
from jax.sharding import PartitionSpec as P

D = 8192
HD = 128
STEPS = 4
GQA = 8
REQUESTS = 8
SOURCES = 128
PIECE = 64
TP = 8
CTX = 16
HEAD_ROWS = STEPS * GQA

ROPE_BASE = 500000.0
ROPE_FACTOR = 8.0
LOW_FACTOR = 1.0
HIGH_FACTOR = 4.0
ROPE_ANCHOR = 8192.0
NEGATIVE = -1e30
SCALE = HD ** (-0.5)


def angles(positions, width):
    base_freq = ROPE_BASE ** (-(2.0 * jnp.arange(width // 2, dtype=jnp.float32)) / width)
    wavelength = 2.0 * math.pi / base_freq
    blend = (ROPE_ANCHOR / wavelength - LOW_FACTOR) / (HIGH_FACTOR - LOW_FACTOR)
    middle = (1.0 - blend) * base_freq / ROPE_FACTOR + blend * base_freq
    freq = jnp.where(
        wavelength > ROPE_ANCHOR / LOW_FACTOR,
        base_freq / ROPE_FACTOR,
        jnp.where(wavelength < ROPE_ANCHOR / HIGH_FACTOR, base_freq, middle),
    )
    return positions.astype(jnp.float32)[..., None] * freq


COLUMNS = (GQA + 2) * HD
SIDE = 4


def partial_kernel(x_ref, hidden_ref, gain_ref, w_ref, *out_refs):
    rows = STEPS * REQUESTS
    share = rows // SIDE
    target = lax.broadcasted_iota(jnp.int32, (rows, rows), 0)
    origin = lax.broadcasted_iota(jnp.int32, (rows, rows), 1)
    receiver = jnp.bitwise_xor(target // share, x_ref[0])
    request = receiver * (REQUESTS // SIDE) + target % share // STEPS
    moves = jnp.where(origin == target % STEPS * REQUESTS + request, 1.0, 0.0)
    values = jnp.dot(
        moves.astype(jnp.bfloat16), hidden_ref[...], preferred_element_type=jnp.float32
    )
    square = jnp.sum(values * values, axis=1, keepdims=True)
    gain = gain_ref[...].astype(jnp.float32).reshape(1, -1)
    scaled = (values * gain).astype(jnp.bfloat16)
    proj = jnp.dot(scaled, w_ref[...], preferred_element_type=jnp.float32)
    square = jnp.broadcast_to(square, (rows, HD))
    for index, out_ref in enumerate(out_refs):
        out_ref[:, pl.ds(0, COLUMNS)] = proj[index * share:(index + 1) * share]
        out_ref[:, pl.ds(COLUMNS, HD)] = square[index * share:(index + 1) * share]


def partial_projection(x, hidden_states, norm_gain, w_qkv):
    vmem = pl.BlockSpec(memory_space=pltpu.VMEM)
    shape = jax.ShapeDtypeStruct((STEPS * REQUESTS // SIDE, COLUMNS + HD), jnp.float32)
    return pl.pallas_call(
        partial_kernel,
        in_specs=[pl.BlockSpec(memory_space=pltpu.SMEM), vmem, vmem, vmem],
        out_specs=[vmem] * SIDE,
        out_shape=[shape] * SIDE,
        compiler_params=pltpu.CompilerParams(vmem_limit_bytes=8 * 1024 * 1024),
        name="partial_projection",
    )(x.reshape(1), hidden_states, norm_gain, w_qkv)


def swap(value, axis, other):
    pairs = [(index, index ^ other) for index in range(lax.axis_size(axis))]
    return lax.ppermute(value, axis, pairs)


def prep_kernel(kv_ref, out_ref, held, ready, in_sems, head_sems, out_sems):
    def fetch(receiver):
        return pltpu.make_async_copy(
            kv_ref.at[receiver], held.at[receiver // 2], in_sems.at[receiver // 2]
        )

    def fetch_head(receiver, head):
        return pltpu.make_async_copy(
            kv_ref.at[receiver, :, :, pl.ds(head * HD, HD)],
            ready.at[receiver, head],
            head_sems.at[receiver // 2, head],
        )

    def place(receiver):
        return pltpu.make_async_copy(
            ready.at[receiver], out_ref.at[receiver], out_sems.at[receiver]
        )

    for receiver in range(0, CTX, 2):
        fetch(receiver).start()
        for head in range(TP):
            fetch_head(receiver + 1, head).start()
    for receiver in range(0, CTX, 2):
        fetch(receiver).wait()
        for head in range(TP):
            ready[receiver, head] = held[receiver // 2, :, :, pl.ds(head * HD, HD)]
        place(receiver).start()
        for head in range(TP):
            fetch_head(receiver + 1, head).wait()
        place(receiver + 1).start()
    for receiver in range(CTX):
        place(receiver).wait()


def prep(kv_cache):
    split = kv_cache.reshape(CTX, PIECE, 2, TP * HD)
    return pl.pallas_call(
        prep_kernel,
        out_shape=jax.ShapeDtypeStruct((CTX, TP, PIECE, 2, HD), jnp.bfloat16),
        in_specs=[pl.BlockSpec(memory_space=pl.ANY)],
        out_specs=pl.BlockSpec(memory_space=pl.ANY),
        scratch_shapes=[
            pltpu.VMEM((CTX // 2, PIECE, 2, TP * HD), jnp.bfloat16),
            pltpu.VMEM((CTX, TP, PIECE, 2, HD), jnp.bfloat16),
            pltpu.SemaphoreType.DMA((CTX // 2,)),
            pltpu.SemaphoreType.DMA((CTX // 2, TP)),
            pltpu.SemaphoreType.DMA((CTX,)),
        ],
        compiler_params=pltpu.CompilerParams(vmem_limit_bytes=56 * 1024 * 1024),
        cost_estimate=pl.CostEstimate(
            flops=0, transcendentals=0, bytes_accessed=4 * kv_cache.size
        ),
        name="cache_by_receiver",
    )(split)


CHUNKS = 4
CHUNK_CTX = CTX // CHUNKS
CHUNK_SOURCES = SOURCES // CHUNKS
CHUNK_KEYS = CHUNK_SOURCES * PIECE
CHUNK_ROWS = CHUNK_KEYS * 2
STATE_ROWS = HEAD_ROWS + 16


def attend_kernel(
    info_ref, kv_ref, own_ref, first_ref, second_ref, third_ref, cos_ref, sin_ref,
    kv_out_ref, out_ref,
    held, wide, pairs, query, scores, peaks, top, total, acc, in_sems, out_sems,
):
    length = info_ref[0]
    part = info_ref[1]
    left = length - part * PIECE

    def fetch(ctx):
        return pltpu.make_async_copy(kv_ref.at[ctx], held.at[ctx], in_sems.at[ctx])

    def place(ctx):
        return pltpu.make_async_copy(held.at[ctx], kv_out_ref.at[ctx], out_sems.at[ctx])

    for ctx in range(CTX):
        fetch(ctx).start()

    row = lax.broadcasted_iota(jnp.int32, (HEAD_ROWS, HD), 0)
    lane = lax.broadcasted_iota(jnp.int32, (HEAD_ROWS, HD), 1)
    slot = lane // PIECE * (2 * PIECE) + lane % PIECE

    summed = own_ref[...] + first_ref[...] + second_ref[...] + third_ref[...]
    norm = lax.rsqrt(summed[:, COLUMNS:] / D + 1e-05)

    def head(index):
        return summed[:, index * HD:(index + 1) * HD] * norm

    def turn(vec):
        return vec * cos_ref[...] + pltpu.roll(vec, HD // 2, 1) * sin_ref[...]

    query[...] = jnp.concatenate([turn(head(g)) for g in range(GQA)], axis=0).astype(jnp.bfloat16)
    rest = jnp.zeros((HD - STEPS, HD), jnp.float32)
    keys = jnp.concatenate([turn(head(GQA)), rest], axis=0).astype(jnp.bfloat16)
    values = jnp.concatenate([head(GQA + 1), rest], axis=0).astype(jnp.bfloat16)
    fresh = lax.dot_general(
        query[...], keys, (((1,), (1,)), ((), ())), preferred_element_type=jnp.float32
    ) * SCALE
    live = jnp.logical_and(lane <= row % STEPS, part == 0)
    fresh = jnp.where(live, fresh, NEGATIVE)
    high = jnp.max(fresh, axis=1, keepdims=True)
    weight = jnp.where(live, jnp.exp(fresh - high), 0.0)
    top[...] = jnp.broadcast_to(high, (HEAD_ROWS, HD))
    total[...] = weight
    acc[...] = jnp.dot(weight.astype(jnp.bfloat16), values, preferred_element_type=jnp.float32)

    def arrive(chunk):
        for ctx in range(chunk * CHUNK_CTX, (chunk + 1) * CHUNK_CTX):
            fetch(ctx).wait()
            place(ctx).start()

    def score(chunk):
        wide[...] = held[pl.ds(chunk * CHUNK_CTX, CHUNK_CTX)].reshape(CHUNK_ROWS, HD).astype(
            jnp.float32
        )
        for index in range(2):
            pairs[chunk % 2, index] = wide[pl.ds(index, CHUNK_KEYS, stride=2), :].astype(
                jnp.bfloat16
            )
        found = lax.dot_general(
            query[...],
            pairs[chunk % 2, 0],
            (((1,), (1,)), ((), ())),
            preferred_element_type=jnp.float32,
        )
        peak = None
        for index in range(CHUNK_KEYS // HD):
            source = chunk * CHUNK_SOURCES + index * 2
            piece = found[:, index * HD:(index + 1) * HD] * SCALE
            piece = jnp.where(slot < left - source * (2 * PIECE), piece, NEGATIVE)
            scores[chunk % 2, :, pl.ds(index * HD, HD)] = piece
            peak = piece if peak is None else jnp.maximum(peak, piece)
        peaks[chunk % 2] = peak

    def fold(chunk):
        high = jnp.maximum(top[...], jnp.max(peaks[chunk % 2], axis=1, keepdims=True))
        fade = jnp.exp(top[...] - high)
        summed = total[...] * fade
        pieces = []
        for index in range(CHUNK_KEYS // HD):
            weight = jnp.exp(scores[chunk % 2, :, pl.ds(index * HD, HD)] - high)
            summed = summed + weight
            pieces.append(weight.astype(jnp.bfloat16))
        top[...] = high
        total[...] = summed
        acc[...] = acc[...] * fade + jnp.dot(
            jnp.concatenate(pieces, axis=1),
            pairs[chunk % 2, 1],
            preferred_element_type=jnp.float32,
        )

    arrive(0)

    @pl.when(left > 0)
    def _():
        score(0)

    for chunk in range(CHUNKS):
        if chunk + 1 < CHUNKS:
            arrive(chunk + 1)

        @pl.when(chunk * CHUNK_SOURCES * 2 * PIECE < left)
        def _(chunk=chunk):
            if chunk + 1 < CHUNKS:
                score(chunk + 1)
            fold(chunk)

    count = jnp.sum(total[...], axis=1, keepdims=True)
    some = count > 0.0
    safe = jnp.where(some, count, 1.0)
    out_ref[pl.ds(0, HEAD_ROWS), :] = (acc[...] / safe).astype(jnp.bfloat16)
    level = jnp.where(some, top[...] + jnp.log(safe), NEGATIVE)
    level = jnp.sum(jnp.where(row == lane, level, 0.0), axis=0, keepdims=True)
    first = level.astype(jnp.bfloat16).astype(jnp.float32)
    second = (level - first).astype(jnp.bfloat16).astype(jnp.float32)
    third = level - first - second
    place_in = lax.broadcasted_iota(jnp.int32, (16, HD), 0)
    parts = jnp.where(place_in == 0, first, jnp.where(place_in == 1, second, third))
    out_ref[pl.ds(HEAD_ROWS, 16), :] = parts.astype(jnp.bfloat16)

    for ctx in range(CTX):
        place(ctx).wait()


def attend(info, moved, sums, cosine, sine):
    anywhere = pl.BlockSpec(memory_space=pl.ANY)
    vmem = pl.BlockSpec(memory_space=pltpu.VMEM)
    return pl.pallas_call(
        attend_kernel,
        in_specs=[pl.BlockSpec(memory_space=pltpu.SMEM), anywhere] + [vmem] * 6,
        out_specs=[anywhere, vmem],
        scratch_shapes=[
            pltpu.VMEM((CTX, TP, 2 * PIECE, HD), jnp.bfloat16),
            pltpu.VMEM((CHUNK_ROWS, HD), jnp.float32),
            pltpu.VMEM((2, 2, CHUNK_KEYS, HD), jnp.bfloat16),
            pltpu.VMEM((HEAD_ROWS, HD), jnp.bfloat16),
            pltpu.VMEM((2, HEAD_ROWS, CHUNK_KEYS), jnp.float32),
            pltpu.VMEM((2, HEAD_ROWS, HD), jnp.float32),
            pltpu.VMEM((HEAD_ROWS, HD), jnp.float32),
            pltpu.VMEM((HEAD_ROWS, HD), jnp.float32),
            pltpu.VMEM((HEAD_ROWS, HD), jnp.float32),
            pltpu.SemaphoreType.DMA((CTX,)),
            pltpu.SemaphoreType.DMA((CTX,)),
        ],
        out_shape=[
            jax.ShapeDtypeStruct((CTX, TP, 2 * PIECE, HD), jnp.bfloat16),
            jax.ShapeDtypeStruct((STATE_ROWS, HD), jnp.bfloat16),
        ],
        compiler_params=pltpu.CompilerParams(vmem_limit_bytes=24 * 1024 * 1024),
        name="attend",
    )(info, moved, *sums, cosine, sine)


def project_kernel(own_states_ref, mate_states_ref, own_ref, mate_ref, out_ref):
    row = lax.broadcasted_iota(jnp.int32, (HEAD_ROWS, HD), 0)
    lane = lax.broadcasted_iota(jnp.int32, (HEAD_ROWS, HD), 1)
    many = REQUESTS * HEAD_ROWS
    target = lax.broadcasted_iota(jnp.int32, (many, many), 0)
    origin = lax.broadcasted_iota(jnp.int32, (many, many), 1)
    head = target // (STEPS * REQUESTS)
    step = target // REQUESTS % STEPS
    request = target % REQUESTS
    moves = jnp.where(origin == request * HEAD_ROWS + head * STEPS + step, 1.0, 0.0)
    moves = moves.astype(jnp.bfloat16)
    totals = []
    for states_ref, w_ref in ((own_states_ref, own_ref), (mate_states_ref, mate_ref)):
        rows = []
        for request in range(REQUESTS):
            spots = [2 * request + part for part in range(2)]
            levels = []
            for spot in spots:
                coded = states_ref[spot, pl.ds(HEAD_ROWS, 16), :].astype(jnp.float32)
                level = coded[0:1] + coded[1:2] + coded[2:3]
                levels.append(jnp.sum(jnp.where(row == lane, level, 0.0), axis=1, keepdims=True))
            high = jnp.maximum(levels[0], levels[1])
            shares = [jnp.exp(level - high) for level in levels]
            whole = shares[0] + shares[1]
            mixed = sum(
                states_ref[spot, pl.ds(0, HEAD_ROWS), :].astype(jnp.float32) * (share / whole)
                for spot, share in zip(spots, shares)
            )
            rows.append(mixed.astype(jnp.bfloat16))
        attn = jnp.dot(
            moves, jnp.concatenate(rows, axis=0), preferred_element_type=jnp.float32
        ).astype(jnp.bfloat16)
        total = jnp.zeros(out_ref.shape, jnp.float32)
        for index in range(GQA):
            total = total + jnp.dot(
                attn[index * HEAD_ROWS:(index + 1) * HEAD_ROWS],
                w_ref[pl.ds(index * HD, HD), :],
                preferred_element_type=jnp.float32,
            )
        totals.append(total)
    out_ref[...] = (totals[0] + totals[1]).astype(jnp.bfloat16)


def project(states, mate_states, w_own, w_mate):
    vmem = pl.BlockSpec(memory_space=pltpu.VMEM)
    return pl.pallas_call(
        project_kernel,
        in_specs=[vmem] * 4,
        out_specs=vmem,
        out_shape=jax.ShapeDtypeStruct((STEPS * REQUESTS, w_own.shape[1]), jnp.bfloat16),
        compiler_params=pltpu.CompilerParams(vmem_limit_bytes=8 * 1024 * 1024),
        name="project",
    )(states, mate_states, w_own, w_mate)


def per_device(hidden_states, norm_gain, prompt_lengths, kv_cache, w_qkv, w_out):
    x = lax.axis_index("x")
    y = lax.axis_index("y")
    mine = x * (REQUESTS // SIDE) + y // 2
    part = y % 2
    length = lax.dynamic_index_in_dim(prompt_lengths, mine, 0, keepdims=False)

    ready = prep(kv_cache).reshape(CTX * TP, 2 * PIECE, HD)
    everyone = ("x", "y", "z", "core")
    moved = lax.all_to_all(ready, everyone, split_axis=0, concat_axis=0, tiled=True)
    moved = moved.reshape(CTX, TP, 2 * PIECE, HD)

    _, hidden_states = lax.optimization_barrier((ready, hidden_states))
    packed = partial_projection(x, hidden_states, norm_gain, w_qkv)
    packed, w_out = lax.optimization_barrier((packed, w_out))
    along_x = packed[0] + sum(swap(packed[k], "x", k) for k in range(1, SIDE))
    w_mate = swap(w_out, "core", 1)
    along_x = along_x.reshape(2, STEPS, COLUMNS + HD)
    own = lax.dynamic_index_in_dim(along_x, y // 2, 0, keepdims=False)
    far = lax.dynamic_index_in_dim(along_x, 1 - y // 2, 0, keepdims=False)
    sums = [own, swap(own, "y", 1), swap(far, "y", 2), swap(far, "y", 3)]

    angle = angles(length + jnp.arange(STEPS, dtype=jnp.int32), HD)
    cosine = jnp.cos(angle)
    sine = jnp.sin(angle)
    cosine = jnp.concatenate([cosine, cosine], axis=1)
    sine = jnp.concatenate([-sine, sine], axis=1)
    info = jnp.stack([length, part]).astype(jnp.int32)
    kv_decode, state = attend(info, moved, sums, cosine, sine)
    kv_decode = kv_decode.reshape(1, SOURCES, PIECE, 2, HD)

    states = jnp.broadcast_to(state[None], (CTX, STATE_ROWS, HD))
    states = lax.all_to_all(states, ("x", "y"), split_axis=0, concat_axis=0, tiled=True)
    out = project(states, swap(states, "core", 1), w_out, w_mate)
    pairs = [(z * 2 + c, (z ^ (1 + 2 * c)) * 2 + c) for z in range(SIDE) for c in range(2)]
    near = lax.ppermute(out, ("z", "core"), pairs)
    across = swap(out, "z", 2)
    shared = swap(near, "core", 1)
    first = lax.axis_index("core") == 0
    one = jnp.where(first, near, shared).astype(jnp.float32)
    three = jnp.where(first, shared, near).astype(jnp.float32)
    block_out = (out.astype(jnp.float32) + one) + (across.astype(jnp.float32) + three)
    block_out = block_out.astype(jnp.bfloat16)
    return (block_out, kv_decode)


def solution(mesh):
    fine = jax.sharding.Mesh(
        mesh.devices.reshape(SIDE, SIDE, SIDE, 2), ("x", "y", "z", "core")
    )
    ctx, tp = ("x", "y"), ("z", "core")
    return jax.shard_map(
        per_device,
        mesh=fine,
        in_specs=(
            P(None, ctx),
            P(ctx),
            P(),
            P(None, ctx + tp, None, None),
            P(ctx, tp),
            P(tp, ctx),
        ),
        out_specs=(P(None, ctx), P(ctx, None, None, None, tp)),
        check_vma=False,
    )
```

```python
import math

import jax
import jax.numpy as jnp
from jax import lax
from jax.experimental import pallas as pl
from jax.experimental.pallas import tpu as pltpu
from jax.sharding import PartitionSpec as P

D = 8192
HD = 128
STEPS = 4
GQA = 8
REQUESTS = 8
SOURCES = 128
PIECE = 64
TP = 8
CTX = 16
HEAD_ROWS = STEPS * GQA

ROPE_BASE = 500000.0
ROPE_FACTOR = 8.0
LOW_FACTOR = 1.0
HIGH_FACTOR = 4.0
ROPE_ANCHOR = 8192.0
NEGATIVE = -1e30
SCALE = HD ** (-0.5)


def angles(positions, width):
    base_freq = ROPE_BASE ** (-(2.0 * jnp.arange(width // 2, dtype=jnp.float32)) / width)
    wavelength = 2.0 * math.pi / base_freq
    blend = (ROPE_ANCHOR / wavelength - LOW_FACTOR) / (HIGH_FACTOR - LOW_FACTOR)
    middle = (1.0 - blend) * base_freq / ROPE_FACTOR + blend * base_freq
    freq = jnp.where(
        wavelength > ROPE_ANCHOR / LOW_FACTOR,
        base_freq / ROPE_FACTOR,
        jnp.where(wavelength < ROPE_ANCHOR / HIGH_FACTOR, base_freq, middle),
    )
    return positions.astype(jnp.float32)[..., None] * freq


COLUMNS = (GQA + 2) * HD
SIDE = 4


def partial_kernel(x_ref, hidden_ref, gain_ref, w_ref, *out_refs):
    rows = STEPS * REQUESTS
    share = rows // SIDE
    target = lax.broadcasted_iota(jnp.int32, (rows, rows), 0)
    origin = lax.broadcasted_iota(jnp.int32, (rows, rows), 1)
    receiver = jnp.bitwise_xor(target // share, x_ref[0])
    request = receiver * (REQUESTS // SIDE) + target % share // STEPS
    moves = jnp.where(origin == target % STEPS * REQUESTS + request, 1.0, 0.0)
    values = jnp.dot(
        moves.astype(jnp.bfloat16), hidden_ref[...], preferred_element_type=jnp.float32
    )
    square = jnp.sum(values * values, axis=1, keepdims=True)
    gain = gain_ref[...].astype(jnp.float32).reshape(1, -1)
    scaled = (values * gain).astype(jnp.bfloat16)
    proj = jnp.dot(scaled, w_ref[...], preferred_element_type=jnp.float32)
    square = jnp.broadcast_to(square, (rows, HD))
    for index, out_ref in enumerate(out_refs):
        out_ref[:, pl.ds(0, COLUMNS)] = proj[index * share:(index + 1) * share]
        out_ref[:, pl.ds(COLUMNS, HD)] = square[index * share:(index + 1) * share]


def partial_projection(x, hidden_states, norm_gain, w_qkv):
    vmem = pl.BlockSpec(memory_space=pltpu.VMEM)
    shape = jax.ShapeDtypeStruct((STEPS * REQUESTS // SIDE, COLUMNS + HD), jnp.float32)
    return pl.pallas_call(
        partial_kernel,
        in_specs=[pl.BlockSpec(memory_space=pltpu.SMEM), vmem, vmem, vmem],
        out_specs=[vmem] * SIDE,
        out_shape=[shape] * SIDE,
        compiler_params=pltpu.CompilerParams(vmem_limit_bytes=8 * 1024 * 1024),
        name="partial_projection",
    )(x.reshape(1), hidden_states, norm_gain, w_qkv)


def swap(value, axis, other):
    pairs = [(index, index ^ other) for index in range(lax.axis_size(axis))]
    return lax.ppermute(value, axis, pairs)


def prep_kernel(kv_ref, out_ref, held, ready, in_sems, head_sems, out_sems):
    def fetch(receiver):
        return pltpu.make_async_copy(
            kv_ref.at[receiver], held.at[receiver // 2], in_sems.at[receiver // 2]
        )

    def fetch_head(receiver, head):
        return pltpu.make_async_copy(
            kv_ref.at[receiver, :, :, pl.ds(head * HD, HD)],
            ready.at[receiver, head],
            head_sems.at[receiver // 2, head],
        )

    def place(receiver):
        return pltpu.make_async_copy(
            ready.at[receiver], out_ref.at[receiver], out_sems.at[receiver]
        )

    for receiver in range(0, CTX, 2):
        fetch(receiver).start()
        for head in range(TP):
            fetch_head(receiver + 1, head).start()
    for receiver in range(0, CTX, 2):
        fetch(receiver).wait()
        for head in range(TP):
            ready[receiver, head] = held[receiver // 2, :, :, pl.ds(head * HD, HD)]
        place(receiver).start()
        for head in range(TP):
            fetch_head(receiver + 1, head).wait()
        place(receiver + 1).start()
    for receiver in range(CTX):
        place(receiver).wait()


def prep(kv_cache):
    split = kv_cache.reshape(CTX, PIECE, 2, TP * HD)
    return pl.pallas_call(
        prep_kernel,
        out_shape=jax.ShapeDtypeStruct((CTX, TP, PIECE, 2, HD), jnp.bfloat16),
        in_specs=[pl.BlockSpec(memory_space=pl.ANY)],
        out_specs=pl.BlockSpec(memory_space=pl.ANY),
        scratch_shapes=[
            pltpu.VMEM((CTX // 2, PIECE, 2, TP * HD), jnp.bfloat16),
            pltpu.VMEM((CTX, TP, PIECE, 2, HD), jnp.bfloat16),
            pltpu.SemaphoreType.DMA((CTX // 2,)),
            pltpu.SemaphoreType.DMA((CTX // 2, TP)),
            pltpu.SemaphoreType.DMA((CTX,)),
        ],
        compiler_params=pltpu.CompilerParams(vmem_limit_bytes=56 * 1024 * 1024),
        cost_estimate=pl.CostEstimate(
            flops=0, transcendentals=0, bytes_accessed=4 * kv_cache.size
        ),
        name="cache_by_receiver",
    )(split)


CHUNKS = 4
CHUNK_CTX = CTX // CHUNKS
CHUNK_SOURCES = SOURCES // CHUNKS
CHUNK_KEYS = CHUNK_SOURCES * PIECE
CHUNK_ROWS = CHUNK_KEYS * 2
STATE_ROWS = HEAD_ROWS + 16


def attend_kernel(
    info_ref, kv_ref, own_ref, first_ref, second_ref, third_ref, cos_ref, sin_ref,
    kv_out_ref, out_ref,
    held, wide, pairs, query, scores, peaks, top, total, acc, in_sems, out_sems,
):
    length = info_ref[0]
    part = info_ref[1]
    left = length - part * PIECE

    def fetch(ctx):
        return pltpu.make_async_copy(kv_ref.at[ctx], held.at[ctx], in_sems.at[ctx])

    def place(ctx):
        return pltpu.make_async_copy(held.at[ctx], kv_out_ref.at[ctx], out_sems.at[ctx])

    for ctx in range(CTX):
        fetch(ctx).start()

    row = lax.broadcasted_iota(jnp.int32, (HEAD_ROWS, HD), 0)
    lane = lax.broadcasted_iota(jnp.int32, (HEAD_ROWS, HD), 1)
    slot = lane // PIECE * (2 * PIECE) + lane % PIECE

    summed = own_ref[...] + first_ref[...] + second_ref[...] + third_ref[...]
    norm = lax.rsqrt(summed[:, COLUMNS:] / D + 1e-05)

    def head(index):
        return summed[:, index * HD:(index + 1) * HD] * norm

    def turn(vec):
        return vec * cos_ref[...] + pltpu.roll(vec, HD // 2, 1) * sin_ref[...]

    query[...] = jnp.concatenate([turn(head(g)) for g in range(GQA)], axis=0).astype(jnp.bfloat16)
    rest = jnp.zeros((HD - STEPS, HD), jnp.float32)
    keys = jnp.concatenate([turn(head(GQA)), rest], axis=0).astype(jnp.bfloat16)
    values = jnp.concatenate([head(GQA + 1), rest], axis=0).astype(jnp.bfloat16)
    fresh = lax.dot_general(
        query[...], keys, (((1,), (1,)), ((), ())), preferred_element_type=jnp.float32
    ) * SCALE
    live = jnp.logical_and(lane <= row % STEPS, part == 0)
    fresh = jnp.where(live, fresh, NEGATIVE)
    high = jnp.max(fresh, axis=1, keepdims=True)
    weight = jnp.where(live, jnp.exp(fresh - high), 0.0)
    top[...] = jnp.broadcast_to(high, (HEAD_ROWS, HD))
    total[...] = weight
    acc[...] = jnp.dot(weight.astype(jnp.bfloat16), values, preferred_element_type=jnp.float32)

    def arrive(chunk):
        for ctx in range(chunk * CHUNK_CTX, (chunk + 1) * CHUNK_CTX):
            fetch(ctx).wait()
            place(ctx).start()

    def score(chunk):
        wide[...] = held[pl.ds(chunk * CHUNK_CTX, CHUNK_CTX)].reshape(CHUNK_ROWS, HD).astype(
            jnp.float32
        )
        for index in range(2):
            pairs[chunk % 2, index] = wide[pl.ds(index, CHUNK_KEYS, stride=2), :].astype(
                jnp.bfloat16
            )
        found = lax.dot_general(
            query[...],
            pairs[chunk % 2, 0],
            (((1,), (1,)), ((), ())),
            preferred_element_type=jnp.float32,
        )
        peak = None
        for index in range(CHUNK_KEYS // HD):
            source = chunk * CHUNK_SOURCES + index * 2
            piece = found[:, index * HD:(index + 1) * HD] * SCALE
            piece = jnp.where(slot < left - source * (2 * PIECE), piece, NEGATIVE)
            scores[chunk % 2, :, pl.ds(index * HD, HD)] = piece
            peak = piece if peak is None else jnp.maximum(peak, piece)
        peaks[chunk % 2] = peak

    def fold(chunk):
        high = jnp.maximum(top[...], jnp.max(peaks[chunk % 2], axis=1, keepdims=True))
        fade = jnp.exp(top[...] - high)
        summed = total[...] * fade
        pieces = []
        for index in range(CHUNK_KEYS // HD):
            weight = jnp.exp(scores[chunk % 2, :, pl.ds(index * HD, HD)] - high)
            summed = summed + weight
            pieces.append(weight.astype(jnp.bfloat16))
        top[...] = high
        total[...] = summed
        acc[...] = acc[...] * fade + jnp.dot(
            jnp.concatenate(pieces, axis=1),
            pairs[chunk % 2, 1],
            preferred_element_type=jnp.float32,
        )

    arrive(0)

    @pl.when(left > 0)
    def _():
        score(0)

    for chunk in range(CHUNKS):
        if chunk + 1 < CHUNKS:
            arrive(chunk + 1)

        @pl.when(chunk * CHUNK_SOURCES * 2 * PIECE < left)
        def _(chunk=chunk):
            if chunk + 1 < CHUNKS:
                score(chunk + 1)
            fold(chunk)

    count = jnp.sum(total[...], axis=1, keepdims=True)
    some = count > 0.0
    safe = jnp.where(some, count, 1.0)
    out_ref[pl.ds(0, HEAD_ROWS), :] = (acc[...] / safe).astype(jnp.bfloat16)
    level = jnp.where(some, top[...] + jnp.log(safe), NEGATIVE)
    level = jnp.sum(jnp.where(row == lane, level, 0.0), axis=0, keepdims=True)
    first = level.astype(jnp.bfloat16).astype(jnp.float32)
    second = (level - first).astype(jnp.bfloat16).astype(jnp.float32)
    third = level - first - second
    place_in = lax.broadcasted_iota(jnp.int32, (16, HD), 0)
    parts = jnp.where(place_in == 0, first, jnp.where(place_in == 1, second, third))
    out_ref[pl.ds(HEAD_ROWS, 16), :] = parts.astype(jnp.bfloat16)

    for ctx in range(CTX):
        place(ctx).wait()


def attend(info, moved, sums, cosine, sine):
    anywhere = pl.BlockSpec(memory_space=pl.ANY)
    vmem = pl.BlockSpec(memory_space=pltpu.VMEM)
    return pl.pallas_call(
        attend_kernel,
        in_specs=[pl.BlockSpec(memory_space=pltpu.SMEM), anywhere] + [vmem] * 6,
        out_specs=[anywhere, vmem],
        scratch_shapes=[
            pltpu.VMEM((CTX, TP, 2 * PIECE, HD), jnp.bfloat16),
            pltpu.VMEM((CHUNK_ROWS, HD), jnp.float32),
            pltpu.VMEM((2, 2, CHUNK_KEYS, HD), jnp.bfloat16),
            pltpu.VMEM((HEAD_ROWS, HD), jnp.bfloat16),
            pltpu.VMEM((2, HEAD_ROWS, CHUNK_KEYS), jnp.float32),
            pltpu.VMEM((2, HEAD_ROWS, HD), jnp.float32),
            pltpu.VMEM((HEAD_ROWS, HD), jnp.float32),
            pltpu.VMEM((HEAD_ROWS, HD), jnp.float32),
            pltpu.VMEM((HEAD_ROWS, HD), jnp.float32),
            pltpu.SemaphoreType.DMA((CTX,)),
            pltpu.SemaphoreType.DMA((CTX,)),
        ],
        out_shape=[
            jax.ShapeDtypeStruct((CTX, TP, 2 * PIECE, HD), jnp.bfloat16),
            jax.ShapeDtypeStruct((STATE_ROWS, HD), jnp.bfloat16),
        ],
        compiler_params=pltpu.CompilerParams(vmem_limit_bytes=24 * 1024 * 1024),
        name="attend",
    )(info, moved, *sums, cosine, sine)


def project_kernel(states_ref, w_ref, *refs):
    base_ref, out_ref = refs if len(refs) == 2 else (None, refs[0])
    row = lax.broadcasted_iota(jnp.int32, (HEAD_ROWS, HD), 0)
    lane = lax.broadcasted_iota(jnp.int32, (HEAD_ROWS, HD), 1)
    many = REQUESTS * HEAD_ROWS
    target = lax.broadcasted_iota(jnp.int32, (many, many), 0)
    origin = lax.broadcasted_iota(jnp.int32, (many, many), 1)
    head = target // (STEPS * REQUESTS)
    step = target // REQUESTS % STEPS
    request = target % REQUESTS
    moves = jnp.where(origin == request * HEAD_ROWS + head * STEPS + step, 1.0, 0.0)
    rows = []
    for request in range(REQUESTS):
        spots = [2 * request + part for part in range(2)]
        levels = []
        for spot in spots:
            coded = states_ref[spot, pl.ds(HEAD_ROWS, 16), :].astype(jnp.float32)
            level = coded[0:1] + coded[1:2] + coded[2:3]
            levels.append(jnp.sum(jnp.where(row == lane, level, 0.0), axis=1, keepdims=True))
        high = jnp.maximum(levels[0], levels[1])
        shares = [jnp.exp(level - high) for level in levels]
        whole = shares[0] + shares[1]
        mixed = sum(
            states_ref[spot, pl.ds(0, HEAD_ROWS), :].astype(jnp.float32) * (share / whole)
            for spot, share in zip(spots, shares)
        )
        rows.append(mixed.astype(jnp.bfloat16))
    attn = jnp.dot(
        moves.astype(jnp.bfloat16),
        jnp.concatenate(rows, axis=0),
        preferred_element_type=jnp.float32,
    ).astype(jnp.bfloat16)
    total = jnp.zeros(out_ref.shape, jnp.float32)
    for index in range(GQA):
        total = total + jnp.dot(
            attn[index * HEAD_ROWS:(index + 1) * HEAD_ROWS],
            w_ref[pl.ds(index * HD, HD), :],
            preferred_element_type=jnp.float32,
        )
    if base_ref is not None:
        total = total + base_ref[...]
    out_ref[...] = total.astype(out_ref.dtype)


def project(states, w, base=None):
    vmem = pl.BlockSpec(memory_space=pltpu.VMEM)
    operands = (states, w) if base is None else (states, w, base)
    kind = jnp.float32 if base is None else jnp.bfloat16
    return pl.pallas_call(
        project_kernel,
        in_specs=[vmem] * len(operands),
        out_specs=vmem,
        out_shape=jax.ShapeDtypeStruct((STEPS * REQUESTS, w.shape[1]), kind),
        compiler_params=pltpu.CompilerParams(vmem_limit_bytes=8 * 1024 * 1024),
        name="project",
    )(*operands)


def per_device(hidden_states, norm_gain, prompt_lengths, kv_cache, w_qkv, w_out):
    x = lax.axis_index("x")
    y = lax.axis_index("y")
    mine = x * (REQUESTS // SIDE) + y // 2
    part = y % 2
    length = lax.dynamic_index_in_dim(prompt_lengths, mine, 0, keepdims=False)

    ready = prep(kv_cache).reshape(CTX * TP, 2 * PIECE, HD)
    everyone = ("x", "y", "z", "core")
    moved = lax.all_to_all(ready, everyone, split_axis=0, concat_axis=0, tiled=True)
    moved = moved.reshape(CTX, TP, 2 * PIECE, HD)

    _, hidden_states = lax.optimization_barrier((ready, hidden_states))
    packed = partial_projection(x, hidden_states, norm_gain, w_qkv)
    packed, w_out = lax.optimization_barrier((packed, w_out))
    along_x = packed[0] + sum(swap(packed[k], "x", k) for k in range(1, SIDE))
    w_mate = swap(w_out, "core", 1)
    along_x = along_x.reshape(2, STEPS, COLUMNS + HD)
    own = lax.dynamic_index_in_dim(along_x, y // 2, 0, keepdims=False)
    far = lax.dynamic_index_in_dim(along_x, 1 - y // 2, 0, keepdims=False)
    sums = [own, swap(own, "y", 1), swap(far, "y", 3), swap(far, "y", 2)]

    angle = angles(length + jnp.arange(STEPS, dtype=jnp.int32), HD)
    cosine = jnp.cos(angle)
    sine = jnp.sin(angle)
    cosine = jnp.concatenate([cosine, cosine], axis=1)
    sine = jnp.concatenate([-sine, sine], axis=1)
    info = jnp.stack([length, part]).astype(jnp.int32)
    kv_decode, state = attend(info, moved, sums, cosine, sine)
    kv_decode = kv_decode.reshape(1, SOURCES, PIECE, 2, HD)

    states = jnp.broadcast_to(state[None], (CTX, STATE_ROWS, HD))
    states = lax.all_to_all(states, ("x", "y"), split_axis=0, concat_axis=0, tiled=True)
    mate_states = swap(states, "core", 1)
    out = project(mate_states, w_mate, project(states, w_out))
    one, three, two = [swap(out, "z", other).astype(jnp.float32) for other in (1, 3, 2)]
    block_out = ((out.astype(jnp.float32) + one) + (two + three)).astype(jnp.bfloat16)
    return (block_out, kv_decode)


def solution(mesh):
    fine = jax.sharding.Mesh(
        mesh.devices.reshape(SIDE, SIDE, SIDE, 2), ("x", "y", "z", "core")
    )
    ctx, tp = ("x", "y"), ("z", "core")
    return jax.shard_map(
        per_device,
        mesh=fine,
        in_specs=(
            P(None, ctx),
            P(ctx),
            P(),
            P(None, ctx + tp, None, None),
            P(ctx, tp),
            P(tp, ctx),
        ),
        out_specs=(P(None, ctx), P(ctx, None, None, None, tp)),
        check_vma=False,
    )
```

```python
import math

import jax
import jax.numpy as jnp
from jax import lax
from jax.experimental import pallas as pl
from jax.experimental.pallas import tpu as pltpu
from jax.sharding import PartitionSpec as P

D = 8192
HD = 128
STEPS = 4
GQA = 8
REQUESTS = 8
SOURCES = 128
PIECE = 64
TP = 8
CTX = 16
HEAD_ROWS = STEPS * GQA

ROPE_BASE = 500000.0
ROPE_FACTOR = 8.0
LOW_FACTOR = 1.0
HIGH_FACTOR = 4.0
ROPE_ANCHOR = 8192.0
NEGATIVE = -1e30
SCALE = HD ** (-0.5)


def angles(positions, width):
    base_freq = ROPE_BASE ** (-(2.0 * jnp.arange(width // 2, dtype=jnp.float32)) / width)
    wavelength = 2.0 * math.pi / base_freq
    blend = (ROPE_ANCHOR / wavelength - LOW_FACTOR) / (HIGH_FACTOR - LOW_FACTOR)
    middle = (1.0 - blend) * base_freq / ROPE_FACTOR + blend * base_freq
    freq = jnp.where(
        wavelength > ROPE_ANCHOR / LOW_FACTOR,
        base_freq / ROPE_FACTOR,
        jnp.where(wavelength < ROPE_ANCHOR / HIGH_FACTOR, base_freq, middle),
    )
    return positions.astype(jnp.float32)[..., None] * freq


COLUMNS = (GQA + 2) * HD
SIDE = 4


def partial_kernel(x_ref, hidden_ref, gain_ref, w_ref, *out_refs):
    rows = STEPS * REQUESTS
    share = rows // SIDE
    target = lax.broadcasted_iota(jnp.int32, (rows, rows), 0)
    origin = lax.broadcasted_iota(jnp.int32, (rows, rows), 1)
    receiver = jnp.bitwise_xor(target // share, x_ref[0])
    request = receiver * (REQUESTS // SIDE) + target % share // STEPS
    moves = jnp.where(origin == target % STEPS * REQUESTS + request, 1.0, 0.0)
    values = jnp.dot(
        moves.astype(jnp.bfloat16), hidden_ref[...], preferred_element_type=jnp.float32
    )
    square = jnp.sum(values * values, axis=1, keepdims=True)
    gain = gain_ref[...].astype(jnp.float32).reshape(1, -1)
    scaled = (values * gain).astype(jnp.bfloat16)
    proj = jnp.dot(scaled, w_ref[...], preferred_element_type=jnp.float32)
    square = jnp.broadcast_to(square, (rows, HD))
    for index, out_ref in enumerate(out_refs):
        out_ref[:, pl.ds(0, COLUMNS)] = proj[index * share:(index + 1) * share]
        out_ref[:, pl.ds(COLUMNS, HD)] = square[index * share:(index + 1) * share]


def partial_projection(x, hidden_states, norm_gain, w_qkv):
    vmem = pl.BlockSpec(memory_space=pltpu.VMEM)
    shape = jax.ShapeDtypeStruct((STEPS * REQUESTS // SIDE, COLUMNS + HD), jnp.float32)
    return pl.pallas_call(
        partial_kernel,
        in_specs=[pl.BlockSpec(memory_space=pltpu.SMEM), vmem, vmem, vmem],
        out_specs=[vmem] * SIDE,
        out_shape=[shape] * SIDE,
        compiler_params=pltpu.CompilerParams(vmem_limit_bytes=8 * 1024 * 1024),
        name="partial_projection",
    )(x.reshape(1), hidden_states, norm_gain, w_qkv)


def swap(value, axis, other):
    pairs = [(index, index ^ other) for index in range(lax.axis_size(axis))]
    return lax.ppermute(value, axis, pairs)


PARTS = 2


def prep_kernel(kv_ref, out_ref, held, ready, in_sems, out_sems):
    depth = PIECE // PARTS
    heads = TP // PARTS

    def fetch(receiver, part):
        span = pl.ds(part * depth, depth)
        return pltpu.make_async_copy(
            kv_ref.at[receiver, span], held.at[receiver, span], in_sems.at[receiver, part]
        )

    def place(receiver, part):
        span = pl.ds(part * heads, heads)
        return pltpu.make_async_copy(
            ready.at[receiver, span], out_ref.at[receiver, span], out_sems.at[receiver, part]
        )

    every = [(receiver, part) for receiver in range(CTX) for part in range(PARTS)]
    for spot in every:
        fetch(*spot).start()
    for receiver in range(CTX):
        for part in range(PARTS):
            fetch(receiver, part).wait()
        for part in range(PARTS):
            for head in range(part * heads, (part + 1) * heads):
                ready[receiver, head] = held[receiver, :, :, pl.ds(head * HD, HD)]
            place(receiver, part).start()
    for spot in every:
        place(*spot).wait()


def prep(kv_cache):
    split = kv_cache.reshape(CTX, PIECE, 2, TP * HD)
    return pl.pallas_call(
        prep_kernel,
        out_shape=jax.ShapeDtypeStruct((CTX, TP, PIECE, 2, HD), jnp.bfloat16),
        in_specs=[pl.BlockSpec(memory_space=pl.ANY)],
        out_specs=pl.BlockSpec(memory_space=pl.ANY),
        scratch_shapes=[
            pltpu.VMEM((CTX, PIECE, 2, TP * HD), jnp.bfloat16),
            pltpu.VMEM((CTX, TP, PIECE, 2, HD), jnp.bfloat16),
            pltpu.SemaphoreType.DMA((CTX, PARTS)),
            pltpu.SemaphoreType.DMA((CTX, PARTS)),
        ],
        compiler_params=pltpu.CompilerParams(vmem_limit_bytes=56 * 1024 * 1024),
        cost_estimate=pl.CostEstimate(
            flops=0, transcendentals=0, bytes_accessed=4 * kv_cache.size
        ),
        name="cache_by_receiver",
    )(split)


CHUNKS = 4
CHUNK_CTX = CTX // CHUNKS
CHUNK_SOURCES = SOURCES // CHUNKS
CHUNK_KEYS = CHUNK_SOURCES * PIECE
CHUNK_ROWS = CHUNK_KEYS * 2
STATE_ROWS = HEAD_ROWS + 16


def attend_kernel(
    info_ref, kv_ref, own_ref, first_ref, second_ref, third_ref, cos_ref, sin_ref,
    kv_out_ref, out_ref,
    held, wide, pairs, query, scores, peaks, top, total, acc, in_sems, out_sems,
):
    length = info_ref[0]
    part = info_ref[1]
    left = length - part * PIECE

    def fetch(ctx, part):
        span = pl.ds(part * (TP // PARTS), TP // PARTS)
        return pltpu.make_async_copy(
            kv_ref.at[ctx, span], held.at[ctx, span], in_sems.at[ctx, part]
        )

    def place(ctx, part):
        span = pl.ds(part * (TP // PARTS), TP // PARTS)
        return pltpu.make_async_copy(
            held.at[ctx, span], kv_out_ref.at[ctx, span], out_sems.at[ctx, part]
        )

    every = [(ctx, part) for ctx in range(CTX) for part in range(PARTS)]
    for spot in every:
        fetch(*spot).start()

    row = lax.broadcasted_iota(jnp.int32, (HEAD_ROWS, HD), 0)
    lane = lax.broadcasted_iota(jnp.int32, (HEAD_ROWS, HD), 1)
    slot = lane // PIECE * (2 * PIECE) + lane % PIECE

    summed = own_ref[...] + first_ref[...] + second_ref[...] + third_ref[...]
    norm = lax.rsqrt(summed[:, COLUMNS:] / D + 1e-05)

    def head(index):
        return summed[:, index * HD:(index + 1) * HD] * norm

    def turn(vec):
        return vec * cos_ref[...] + pltpu.roll(vec, HD // 2, 1) * sin_ref[...]

    query[...] = jnp.concatenate([turn(head(g)) for g in range(GQA)], axis=0).astype(jnp.bfloat16)
    rest = jnp.zeros((HD - STEPS, HD), jnp.float32)
    keys = jnp.concatenate([turn(head(GQA)), rest], axis=0).astype(jnp.bfloat16)
    values = jnp.concatenate([head(GQA + 1), rest], axis=0).astype(jnp.bfloat16)
    fresh = lax.dot_general(
        query[...], keys, (((1,), (1,)), ((), ())), preferred_element_type=jnp.float32
    ) * SCALE
    live = jnp.logical_and(lane <= row % STEPS, part == 0)
    fresh = jnp.where(live, fresh, NEGATIVE)
    high = jnp.max(fresh, axis=1, keepdims=True)
    weight = jnp.where(live, jnp.exp(fresh - high), 0.0)
    top[...] = jnp.broadcast_to(high, (HEAD_ROWS, HD))
    total[...] = weight
    acc[...] = jnp.dot(weight.astype(jnp.bfloat16), values, preferred_element_type=jnp.float32)

    def arrive(chunk):
        for spot in every[chunk * CHUNK_CTX * PARTS:(chunk + 1) * CHUNK_CTX * PARTS]:
            fetch(*spot).wait()
            place(*spot).start()

    def score(chunk):
        wide[...] = held[pl.ds(chunk * CHUNK_CTX, CHUNK_CTX)].reshape(CHUNK_ROWS, HD).astype(
            jnp.float32
        )
        for index in range(2):
            pairs[chunk % 2, index] = wide[pl.ds(index, CHUNK_KEYS, stride=2), :].astype(
                jnp.bfloat16
            )
        found = lax.dot_general(
            query[...],
            pairs[chunk % 2, 0],
            (((1,), (1,)), ((), ())),
            preferred_element_type=jnp.float32,
        )
        peak = None
        for index in range(CHUNK_KEYS // HD):
            source = chunk * CHUNK_SOURCES + index * 2
            piece = found[:, index * HD:(index + 1) * HD] * SCALE
            piece = jnp.where(slot < left - source * (2 * PIECE), piece, NEGATIVE)
            scores[chunk % 2, :, pl.ds(index * HD, HD)] = piece
            peak = piece if peak is None else jnp.maximum(peak, piece)
        peaks[chunk % 2] = peak

    def fold(chunk):
        high = jnp.maximum(top[...], jnp.max(peaks[chunk % 2], axis=1, keepdims=True))
        fade = jnp.exp(top[...] - high)
        summed = total[...] * fade
        pieces = []
        for index in range(CHUNK_KEYS // HD):
            weight = jnp.exp(scores[chunk % 2, :, pl.ds(index * HD, HD)] - high)
            summed = summed + weight
            pieces.append(weight.astype(jnp.bfloat16))
        top[...] = high
        total[...] = summed
        acc[...] = acc[...] * fade + jnp.dot(
            jnp.concatenate(pieces, axis=1),
            pairs[chunk % 2, 1],
            preferred_element_type=jnp.float32,
        )

    arrive(0)

    @pl.when(left > 0)
    def _():
        score(0)

    for chunk in range(CHUNKS):
        if chunk + 1 < CHUNKS:
            arrive(chunk + 1)

        @pl.when(chunk * CHUNK_SOURCES * 2 * PIECE < left)
        def _(chunk=chunk):
            if chunk + 1 < CHUNKS:
                score(chunk + 1)
            fold(chunk)

    count = jnp.sum(total[...], axis=1, keepdims=True)
    some = count > 0.0
    safe = jnp.where(some, count, 1.0)
    out_ref[pl.ds(0, HEAD_ROWS), :] = (acc[...] / safe).astype(jnp.bfloat16)
    level = jnp.where(some, top[...] + jnp.log(safe), NEGATIVE)
    level = jnp.sum(jnp.where(row == lane, level, 0.0), axis=0, keepdims=True)
    first = level.astype(jnp.bfloat16).astype(jnp.float32)
    second = (level - first).astype(jnp.bfloat16).astype(jnp.float32)
    third = level - first - second
    place_in = lax.broadcasted_iota(jnp.int32, (16, HD), 0)
    parts = jnp.where(place_in == 0, first, jnp.where(place_in == 1, second, third))
    out_ref[pl.ds(HEAD_ROWS, 16), :] = parts.astype(jnp.bfloat16)

    for spot in every:
        place(*spot).wait()


def attend(info, moved, sums, cosine, sine):
    anywhere = pl.BlockSpec(memory_space=pl.ANY)
    vmem = pl.BlockSpec(memory_space=pltpu.VMEM)
    return pl.pallas_call(
        attend_kernel,
        in_specs=[pl.BlockSpec(memory_space=pltpu.SMEM), anywhere] + [vmem] * 6,
        out_specs=[anywhere, vmem],
        scratch_shapes=[
            pltpu.VMEM((CTX, TP, 2 * PIECE, HD), jnp.bfloat16),
            pltpu.VMEM((CHUNK_ROWS, HD), jnp.float32),
            pltpu.VMEM((2, 2, CHUNK_KEYS, HD), jnp.bfloat16),
            pltpu.VMEM((HEAD_ROWS, HD), jnp.bfloat16),
            pltpu.VMEM((2, HEAD_ROWS, CHUNK_KEYS), jnp.float32),
            pltpu.VMEM((2, HEAD_ROWS, HD), jnp.float32),
            pltpu.VMEM((HEAD_ROWS, HD), jnp.float32),
            pltpu.VMEM((HEAD_ROWS, HD), jnp.float32),
            pltpu.VMEM((HEAD_ROWS, HD), jnp.float32),
            pltpu.SemaphoreType.DMA((CTX, PARTS)),
            pltpu.SemaphoreType.DMA((CTX, PARTS)),
        ],
        out_shape=[
            jax.ShapeDtypeStruct((CTX, TP, 2 * PIECE, HD), jnp.bfloat16),
            jax.ShapeDtypeStruct((STATE_ROWS, HD), jnp.bfloat16),
        ],
        compiler_params=pltpu.CompilerParams(vmem_limit_bytes=24 * 1024 * 1024),
        name="attend",
    )(info, moved, *sums, cosine, sine)


def project_kernel(states_ref, w_ref, *refs):
    base_ref, out_ref = refs if len(refs) == 2 else (None, refs[0])
    row = lax.broadcasted_iota(jnp.int32, (HEAD_ROWS, HD), 0)
    lane = lax.broadcasted_iota(jnp.int32, (HEAD_ROWS, HD), 1)
    many = REQUESTS * HEAD_ROWS
    target = lax.broadcasted_iota(jnp.int32, (many, many), 0)
    origin = lax.broadcasted_iota(jnp.int32, (many, many), 1)
    head = target // (STEPS * REQUESTS)
    step = target // REQUESTS % STEPS
    request = target % REQUESTS
    moves = jnp.where(origin == request * HEAD_ROWS + head * STEPS + step, 1.0, 0.0)
    rows = []
    for request in range(REQUESTS):
        spots = [2 * request + part for part in range(2)]
        levels = []
        for spot in spots:
            coded = states_ref[spot, pl.ds(HEAD_ROWS, 16), :].astype(jnp.float32)
            level = coded[0:1] + coded[1:2] + coded[2:3]
            levels.append(jnp.sum(jnp.where(row == lane, level, 0.0), axis=1, keepdims=True))
        high = jnp.maximum(levels[0], levels[1])
        shares = [jnp.exp(level - high) for level in levels]
        whole = shares[0] + shares[1]
        mixed = sum(
            states_ref[spot, pl.ds(0, HEAD_ROWS), :].astype(jnp.float32) * (share / whole)
            for spot, share in zip(spots, shares)
        )
        rows.append(mixed.astype(jnp.bfloat16))
    attn = jnp.dot(
        moves.astype(jnp.bfloat16),
        jnp.concatenate(rows, axis=0),
        preferred_element_type=jnp.float32,
    ).astype(jnp.bfloat16)
    total = jnp.zeros(out_ref.shape, jnp.float32)
    for index in range(GQA):
        total = total + jnp.dot(
            attn[index * HEAD_ROWS:(index + 1) * HEAD_ROWS],
            w_ref[pl.ds(index * HD, HD), :],
            preferred_element_type=jnp.float32,
        )
    if base_ref is not None:
        total = total + base_ref[...]
    out_ref[...] = total.astype(out_ref.dtype)


def project(states, w, base=None):
    vmem = pl.BlockSpec(memory_space=pltpu.VMEM)
    operands = (states, w) if base is None else (states, w, base)
    kind = jnp.float32 if base is None else jnp.bfloat16
    return pl.pallas_call(
        project_kernel,
        in_specs=[vmem] * len(operands),
        out_specs=vmem,
        out_shape=jax.ShapeDtypeStruct((STEPS * REQUESTS, w.shape[1]), kind),
        compiler_params=pltpu.CompilerParams(vmem_limit_bytes=8 * 1024 * 1024),
        name="project",
    )(*operands)


def per_device(hidden_states, norm_gain, prompt_lengths, kv_cache, w_qkv, w_out):
    x = lax.axis_index("x")
    y = lax.axis_index("y")
    mine = x * (REQUESTS // SIDE) + y // 2
    part = y % 2
    length = lax.dynamic_index_in_dim(prompt_lengths, mine, 0, keepdims=False)

    ready = prep(kv_cache).reshape(CTX * TP, 2 * PIECE, HD)
    everyone = ("x", "y", "z", "core")
    moved = lax.all_to_all(ready, everyone, split_axis=0, concat_axis=0, tiled=True)
    moved = moved.reshape(CTX, TP, 2 * PIECE, HD)

    _, hidden_states = lax.optimization_barrier((ready, hidden_states))
    packed = partial_projection(x, hidden_states, norm_gain, w_qkv)
    packed, w_out = lax.optimization_barrier((packed, w_out))
    along_x = packed[0] + sum(swap(packed[k], "x", k) for k in range(1, SIDE))
    w_mate = swap(w_out, "core", 1)
    along_x = along_x.reshape(2, STEPS, COLUMNS + HD)
    own = lax.dynamic_index_in_dim(along_x, y // 2, 0, keepdims=False)
    far = lax.dynamic_index_in_dim(along_x, 1 - y // 2, 0, keepdims=False)
    sums = [own, swap(own, "y", 1), swap(far, "y", 3), swap(far, "y", 2)]

    angle = angles(length + jnp.arange(STEPS, dtype=jnp.int32), HD)
    cosine = jnp.cos(angle)
    sine = jnp.sin(angle)
    cosine = jnp.concatenate([cosine, cosine], axis=1)
    sine = jnp.concatenate([-sine, sine], axis=1)
    info = jnp.stack([length, part]).astype(jnp.int32)
    kv_decode, state = attend(info, moved, sums, cosine, sine)
    kv_decode = kv_decode.reshape(1, SOURCES, PIECE, 2, HD)

    states = jnp.broadcast_to(state[None], (CTX, STATE_ROWS, HD))
    states = lax.all_to_all(states, ("x", "y"), split_axis=0, concat_axis=0, tiled=True)
    mate_states = swap(states, "core", 1)
    out = project(mate_states, w_mate, project(states, w_out))
    pairs = [(z * 2 + c, (z ^ (1 + 2 * c)) * 2 + c) for z in range(SIDE) for c in range(2)]
    near = lax.ppermute(out, ("z", "core"), pairs)
    across = swap(out, "z", 2)
    shared = swap(near, "core", 1)
    first = lax.axis_index("core") == 0
    one = jnp.where(first, near, shared).astype(jnp.float32)
    three = jnp.where(first, shared, near).astype(jnp.float32)
    block_out = (out.astype(jnp.float32) + one) + (across.astype(jnp.float32) + three)
    block_out = block_out.astype(jnp.bfloat16)
    return (block_out, kv_decode)


def solution(mesh):
    fine = jax.sharding.Mesh(
        mesh.devices.reshape(SIDE, SIDE, SIDE, 2), ("x", "y", "z", "core")
    )
    ctx, tp = ("x", "y"), ("z", "core")
    return jax.shard_map(
        per_device,
        mesh=fine,
        in_specs=(
            P(None, ctx),
            P(ctx),
            P(),
            P(None, ctx + tp, None, None),
            P(ctx, tp),
            P(tp, ctx),
        ),
        out_specs=(P(None, ctx), P(ctx, None, None, None, tp)),
        check_vma=False,
    )
```

```python
import math

import jax
import jax.numpy as jnp
from jax import lax
from jax.experimental import pallas as pl
from jax.experimental.pallas import tpu as pltpu
from jax.sharding import PartitionSpec as P

D = 8192
HD = 128
STEPS = 4
GQA = 8
REQUESTS = 8
SOURCES = 128
PIECE = 64
TP = 8
CTX = 16
HEAD_ROWS = STEPS * GQA

ROPE_BASE = 500000.0
ROPE_FACTOR = 8.0
LOW_FACTOR = 1.0
HIGH_FACTOR = 4.0
ROPE_ANCHOR = 8192.0
NEGATIVE = -1e30
SCALE = HD ** (-0.5)


def angles(positions, width):
    base_freq = ROPE_BASE ** (-(2.0 * jnp.arange(width // 2, dtype=jnp.float32)) / width)
    wavelength = 2.0 * math.pi / base_freq
    blend = (ROPE_ANCHOR / wavelength - LOW_FACTOR) / (HIGH_FACTOR - LOW_FACTOR)
    middle = (1.0 - blend) * base_freq / ROPE_FACTOR + blend * base_freq
    freq = jnp.where(
        wavelength > ROPE_ANCHOR / LOW_FACTOR,
        base_freq / ROPE_FACTOR,
        jnp.where(wavelength < ROPE_ANCHOR / HIGH_FACTOR, base_freq, middle),
    )
    return positions.astype(jnp.float32)[..., None] * freq


COLUMNS = (GQA + 2) * HD
SIDE = 4


def partial_kernel(x_ref, hidden_ref, gain_ref, w_ref, *out_refs):
    rows = STEPS * REQUESTS
    share = rows // SIDE
    target = lax.broadcasted_iota(jnp.int32, (rows, rows), 0)
    origin = lax.broadcasted_iota(jnp.int32, (rows, rows), 1)
    receiver = jnp.bitwise_xor(target // share, x_ref[0])
    request = receiver * (REQUESTS // SIDE) + target % share // STEPS
    moves = jnp.where(origin == target % STEPS * REQUESTS + request, 1.0, 0.0)
    values = jnp.dot(
        moves.astype(jnp.bfloat16), hidden_ref[...], preferred_element_type=jnp.float32
    )
    square = jnp.sum(values * values, axis=1, keepdims=True)
    gain = gain_ref[...].astype(jnp.float32).reshape(1, -1)
    scaled = (values * gain).astype(jnp.bfloat16)
    proj = jnp.dot(scaled, w_ref[...], preferred_element_type=jnp.float32)
    square = jnp.broadcast_to(square, (rows, HD))
    for index, out_ref in enumerate(out_refs):
        out_ref[:, pl.ds(0, COLUMNS)] = proj[index * share:(index + 1) * share]
        out_ref[:, pl.ds(COLUMNS, HD)] = square[index * share:(index + 1) * share]


def partial_projection(x, hidden_states, norm_gain, w_qkv):
    vmem = pl.BlockSpec(memory_space=pltpu.VMEM)
    shape = jax.ShapeDtypeStruct((STEPS * REQUESTS // SIDE, COLUMNS + HD), jnp.float32)
    return pl.pallas_call(
        partial_kernel,
        in_specs=[pl.BlockSpec(memory_space=pltpu.SMEM), vmem, vmem, vmem],
        out_specs=[vmem] * SIDE,
        out_shape=[shape] * SIDE,
        compiler_params=pltpu.CompilerParams(vmem_limit_bytes=8 * 1024 * 1024),
        name="partial_projection",
    )(x.reshape(1), hidden_states, norm_gain, w_qkv)


def swap(value, axis, other):
    pairs = [(index, index ^ other) for index in range(lax.axis_size(axis))]
    return lax.ppermute(value, axis, pairs)


GROUP = 2


def prep_kernel(kv_ref, out_ref, held, ready, in_sems, out_sems):
    def fetch(index):
        span = pl.ds(index * GROUP, GROUP)
        return pltpu.make_async_copy(kv_ref.at[span], held.at[span], in_sems.at[index])

    def place(index):
        span = pl.ds(index * GROUP, GROUP)
        return pltpu.make_async_copy(ready.at[span], out_ref.at[span], out_sems.at[index])

    for index in range(CTX // GROUP):
        fetch(index).start()
    for index in range(CTX // GROUP):
        fetch(index).wait()
        for receiver in range(index * GROUP, (index + 1) * GROUP):
            for head in range(TP):
                ready[receiver, head] = held[receiver, :, :, pl.ds(head * HD, HD)]
        place(index).start()
    for index in range(CTX // GROUP):
        place(index).wait()


def prep(kv_cache):
    split = kv_cache.reshape(CTX, PIECE, 2, TP * HD)
    return pl.pallas_call(
        prep_kernel,
        out_shape=jax.ShapeDtypeStruct((CTX, TP, PIECE, 2, HD), jnp.bfloat16),
        in_specs=[pl.BlockSpec(memory_space=pl.ANY)],
        out_specs=pl.BlockSpec(memory_space=pl.ANY),
        scratch_shapes=[
            pltpu.VMEM((CTX, PIECE, 2, TP * HD), jnp.bfloat16),
            pltpu.VMEM((CTX, TP, PIECE, 2, HD), jnp.bfloat16),
            pltpu.SemaphoreType.DMA((CTX // GROUP,)),
            pltpu.SemaphoreType.DMA((CTX // GROUP,)),
        ],
        compiler_params=pltpu.CompilerParams(vmem_limit_bytes=56 * 1024 * 1024),
        cost_estimate=pl.CostEstimate(
            flops=0, transcendentals=0, bytes_accessed=4 * kv_cache.size
        ),
        name="cache_by_receiver",
    )(split)


CHUNKS = 4
CHUNK_CTX = CTX // CHUNKS
CHUNK_SOURCES = SOURCES // CHUNKS
CHUNK_KEYS = CHUNK_SOURCES * PIECE
CHUNK_ROWS = CHUNK_KEYS * 2
STATE_ROWS = HEAD_ROWS + 16


def attend_kernel(
    info_ref, kv_ref, own_ref, first_ref, second_ref, third_ref, cos_ref, sin_ref,
    kv_out_ref, out_ref,
    held, wide, pairs, query, scores, peaks, top, total, acc, in_sems, out_sems,
):
    length = info_ref[0]
    part = info_ref[1]
    left = length - part * PIECE

    def fetch(index):
        span = pl.ds(index * GROUP, GROUP)
        return pltpu.make_async_copy(kv_ref.at[span], held.at[span], in_sems.at[index])

    def place(index):
        span = pl.ds(index * GROUP, GROUP)
        return pltpu.make_async_copy(held.at[span], kv_out_ref.at[span], out_sems.at[index])

    for index in range(CTX // GROUP):
        fetch(index).start()

    row = lax.broadcasted_iota(jnp.int32, (HEAD_ROWS, HD), 0)
    lane = lax.broadcasted_iota(jnp.int32, (HEAD_ROWS, HD), 1)
    slot = lane // PIECE * (2 * PIECE) + lane % PIECE

    summed = own_ref[...] + first_ref[...] + second_ref[...] + third_ref[...]
    norm = lax.rsqrt(summed[:, COLUMNS:] / D + 1e-05)

    def head(index):
        return summed[:, index * HD:(index + 1) * HD] * norm

    def turn(vec):
        return vec * cos_ref[...] + pltpu.roll(vec, HD // 2, 1) * sin_ref[...]

    query[...] = jnp.concatenate([turn(head(g)) for g in range(GQA)], axis=0).astype(jnp.bfloat16)
    rest = jnp.zeros((HD - STEPS, HD), jnp.float32)
    keys = jnp.concatenate([turn(head(GQA)), rest], axis=0).astype(jnp.bfloat16)
    values = jnp.concatenate([head(GQA + 1), rest], axis=0).astype(jnp.bfloat16)
    fresh = lax.dot_general(
        query[...], keys, (((1,), (1,)), ((), ())), preferred_element_type=jnp.float32
    ) * SCALE
    live = jnp.logical_and(lane <= row % STEPS, part == 0)
    fresh = jnp.where(live, fresh, NEGATIVE)
    high = jnp.max(fresh, axis=1, keepdims=True)
    weight = jnp.where(live, jnp.exp(fresh - high), 0.0)
    top[...] = jnp.broadcast_to(high, (HEAD_ROWS, HD))
    total[...] = weight
    acc[...] = jnp.dot(weight.astype(jnp.bfloat16), values, preferred_element_type=jnp.float32)

    def arrive(chunk):
        for index in range(chunk * CHUNK_CTX // GROUP, (chunk + 1) * CHUNK_CTX // GROUP):
            fetch(index).wait()
            place(index).start()

    def score(chunk):
        wide[...] = held[pl.ds(chunk * CHUNK_CTX, CHUNK_CTX)].reshape(CHUNK_ROWS, HD).astype(
            jnp.float32
        )
        for index in range(2):
            pairs[chunk % 2, index] = wide[pl.ds(index, CHUNK_KEYS, stride=2), :].astype(
                jnp.bfloat16
            )
        found = lax.dot_general(
            query[...],
            pairs[chunk % 2, 0],
            (((1,), (1,)), ((), ())),
            preferred_element_type=jnp.float32,
        )
        peak = None
        for index in range(CHUNK_KEYS // HD):
            source = chunk * CHUNK_SOURCES + index * 2
            piece = found[:, index * HD:(index + 1) * HD] * SCALE
            piece = jnp.where(slot < left - source * (2 * PIECE), piece, NEGATIVE)
            scores[chunk % 2, :, pl.ds(index * HD, HD)] = piece
            peak = piece if peak is None else jnp.maximum(peak, piece)
        peaks[chunk % 2] = peak

    def fold(chunk):
        high = jnp.maximum(top[...], jnp.max(peaks[chunk % 2], axis=1, keepdims=True))
        fade = jnp.exp(top[...] - high)
        summed = total[...] * fade
        pieces = []
        for index in range(CHUNK_KEYS // HD):
            weight = jnp.exp(scores[chunk % 2, :, pl.ds(index * HD, HD)] - high)
            summed = summed + weight
            pieces.append(weight.astype(jnp.bfloat16))
        top[...] = high
        total[...] = summed
        acc[...] = acc[...] * fade + jnp.dot(
            jnp.concatenate(pieces, axis=1),
            pairs[chunk % 2, 1],
            preferred_element_type=jnp.float32,
        )

    arrive(0)

    @pl.when(left > 0)
    def _():
        score(0)

    for chunk in range(CHUNKS):
        if chunk + 1 < CHUNKS:
            arrive(chunk + 1)

        @pl.when(chunk * CHUNK_SOURCES * 2 * PIECE < left)
        def _(chunk=chunk):
            if chunk + 1 < CHUNKS:
                score(chunk + 1)
            fold(chunk)

    count = jnp.sum(total[...], axis=1, keepdims=True)
    some = count > 0.0
    safe = jnp.where(some, count, 1.0)
    out_ref[pl.ds(0, HEAD_ROWS), :] = (acc[...] / safe).astype(jnp.bfloat16)
    level = jnp.where(some, top[...] + jnp.log(safe), NEGATIVE)
    level = jnp.sum(jnp.where(row == lane, level, 0.0), axis=0, keepdims=True)
    first = level.astype(jnp.bfloat16).astype(jnp.float32)
    second = (level - first).astype(jnp.bfloat16).astype(jnp.float32)
    third = level - first - second
    place_in = lax.broadcasted_iota(jnp.int32, (16, HD), 0)
    parts = jnp.where(place_in == 0, first, jnp.where(place_in == 1, second, third))
    out_ref[pl.ds(HEAD_ROWS, 16), :] = parts.astype(jnp.bfloat16)

    for index in range(CTX // GROUP):
        place(index).wait()


def attend(info, moved, sums, cosine, sine):
    anywhere = pl.BlockSpec(memory_space=pl.ANY)
    vmem = pl.BlockSpec(memory_space=pltpu.VMEM)
    return pl.pallas_call(
        attend_kernel,
        in_specs=[pl.BlockSpec(memory_space=pltpu.SMEM), anywhere] + [vmem] * 6,
        out_specs=[anywhere, vmem],
        scratch_shapes=[
            pltpu.VMEM((CTX, TP, 2 * PIECE, HD), jnp.bfloat16),
            pltpu.VMEM((CHUNK_ROWS, HD), jnp.float32),
            pltpu.VMEM((2, 2, CHUNK_KEYS, HD), jnp.bfloat16),
            pltpu.VMEM((HEAD_ROWS, HD), jnp.bfloat16),
            pltpu.VMEM((2, HEAD_ROWS, CHUNK_KEYS), jnp.float32),
            pltpu.VMEM((2, HEAD_ROWS, HD), jnp.float32),
            pltpu.VMEM((HEAD_ROWS, HD), jnp.float32),
            pltpu.VMEM((HEAD_ROWS, HD), jnp.float32),
            pltpu.VMEM((HEAD_ROWS, HD), jnp.float32),
            pltpu.SemaphoreType.DMA((CTX // GROUP,)),
            pltpu.SemaphoreType.DMA((CTX // GROUP,)),
        ],
        out_shape=[
            jax.ShapeDtypeStruct((CTX, TP, 2 * PIECE, HD), jnp.bfloat16),
            jax.ShapeDtypeStruct((STATE_ROWS, HD), jnp.bfloat16),
        ],
        compiler_params=pltpu.CompilerParams(vmem_limit_bytes=24 * 1024 * 1024),
        name="attend",
    )(info, moved, *sums, cosine, sine)


def project_kernel(states_ref, w_ref, *refs):
    base_ref, out_ref = refs if len(refs) == 2 else (None, refs[0])
    row = lax.broadcasted_iota(jnp.int32, (HEAD_ROWS, HD), 0)
    lane = lax.broadcasted_iota(jnp.int32, (HEAD_ROWS, HD), 1)
    many = REQUESTS * HEAD_ROWS
    target = lax.broadcasted_iota(jnp.int32, (many, many), 0)
    origin = lax.broadcasted_iota(jnp.int32, (many, many), 1)
    head = target // (STEPS * REQUESTS)
    step = target // REQUESTS % STEPS
    request = target % REQUESTS
    moves = jnp.where(origin == request * HEAD_ROWS + head * STEPS + step, 1.0, 0.0)
    rows = []
    for request in range(REQUESTS):
        spots = [2 * request + part for part in range(2)]
        levels = []
        for spot in spots:
            coded = states_ref[spot, pl.ds(HEAD_ROWS, 16), :].astype(jnp.float32)
            level = coded[0:1] + coded[1:2] + coded[2:3]
            levels.append(jnp.sum(jnp.where(row == lane, level, 0.0), axis=1, keepdims=True))
        high = jnp.maximum(levels[0], levels[1])
        shares = [jnp.exp(level - high) for level in levels]
        whole = shares[0] + shares[1]
        mixed = sum(
            states_ref[spot, pl.ds(0, HEAD_ROWS), :].astype(jnp.float32) * (share / whole)
            for spot, share in zip(spots, shares)
        )
        rows.append(mixed.astype(jnp.bfloat16))
    attn = jnp.dot(
        moves.astype(jnp.bfloat16),
        jnp.concatenate(rows, axis=0),
        preferred_element_type=jnp.float32,
    ).astype(jnp.bfloat16)
    total = jnp.zeros(out_ref.shape, jnp.float32)
    for index in range(GQA):
        total = total + jnp.dot(
            attn[index * HEAD_ROWS:(index + 1) * HEAD_ROWS],
            w_ref[pl.ds(index * HD, HD), :],
            preferred_element_type=jnp.float32,
        )
    if base_ref is not None:
        total = total + base_ref[...]
    out_ref[...] = total.astype(out_ref.dtype)


def project(states, w, base=None):
    vmem = pl.BlockSpec(memory_space=pltpu.VMEM)
    operands = (states, w) if base is None else (states, w, base)
    kind = jnp.float32 if base is None else jnp.bfloat16
    return pl.pallas_call(
        project_kernel,
        in_specs=[vmem] * len(operands),
        out_specs=vmem,
        out_shape=jax.ShapeDtypeStruct((STEPS * REQUESTS, w.shape[1]), kind),
        compiler_params=pltpu.CompilerParams(vmem_limit_bytes=8 * 1024 * 1024),
        name="project",
    )(*operands)


def per_device(hidden_states, norm_gain, prompt_lengths, kv_cache, w_qkv, w_out):
    x = lax.axis_index("x")
    y = lax.axis_index("y")
    mine = x * (REQUESTS // SIDE) + y // 2
    part = y % 2
    length = lax.dynamic_index_in_dim(prompt_lengths, mine, 0, keepdims=False)

    ready = prep(kv_cache).reshape(CTX * TP, 2 * PIECE, HD)
    everyone = ("x", "y", "z", "core")
    moved = lax.all_to_all(ready, everyone, split_axis=0, concat_axis=0, tiled=True)
    moved = moved.reshape(CTX, TP, 2 * PIECE, HD)

    _, hidden_states = lax.optimization_barrier((ready, hidden_states))
    packed = partial_projection(x, hidden_states, norm_gain, w_qkv)
    packed, w_out = lax.optimization_barrier((packed, w_out))
    along_x = packed[0] + sum(swap(packed[k], "x", k) for k in range(1, SIDE))
    w_mate = swap(w_out, "core", 1)
    along_x = along_x.reshape(2, STEPS, COLUMNS + HD)
    own = lax.dynamic_index_in_dim(along_x, y // 2, 0, keepdims=False)
    far = lax.dynamic_index_in_dim(along_x, 1 - y // 2, 0, keepdims=False)
    sums = [own, swap(own, "y", 1), swap(far, "y", 3), swap(far, "y", 2)]

    angle = angles(length + jnp.arange(STEPS, dtype=jnp.int32), HD)
    cosine = jnp.cos(angle)
    sine = jnp.sin(angle)
    cosine = jnp.concatenate([cosine, cosine], axis=1)
    sine = jnp.concatenate([-sine, sine], axis=1)
    info = jnp.stack([length, part]).astype(jnp.int32)
    kv_decode, state = attend(info, moved, sums, cosine, sine)
    kv_decode = kv_decode.reshape(1, SOURCES, PIECE, 2, HD)

    states = jnp.broadcast_to(state[None], (CTX, STATE_ROWS, HD))
    states = lax.all_to_all(states, ("x", "y"), split_axis=0, concat_axis=0, tiled=True)
    mate_states = swap(states, "core", 1)
    out = project(mate_states, w_mate, project(states, w_out))
    pairs = [(z * 2 + c, (z ^ (1 + 2 * c)) * 2 + c) for z in range(SIDE) for c in range(2)]
    near = lax.ppermute(out, ("z", "core"), pairs)
    across = swap(out, "z", 2)
    shared = swap(near, "core", 1)
    first = lax.axis_index("core") == 0
    one = jnp.where(first, near, shared).astype(jnp.float32)
    three = jnp.where(first, shared, near).astype(jnp.float32)
    block_out = (out.astype(jnp.float32) + one) + (across.astype(jnp.float32) + three)
    block_out = block_out.astype(jnp.bfloat16)
    return (block_out, kv_decode)


def solution(mesh):
    fine = jax.sharding.Mesh(
        mesh.devices.reshape(SIDE, SIDE, SIDE, 2), ("x", "y", "z", "core")
    )
    ctx, tp = ("x", "y"), ("z", "core")
    return jax.shard_map(
        per_device,
        mesh=fine,
        in_specs=(
            P(None, ctx),
            P(ctx),
            P(),
            P(None, ctx + tp, None, None),
            P(ctx, tp),
            P(tp, ctx),
        ),
        out_specs=(P(None, ctx), P(ctx, None, None, None, tp)),
        check_vma=False,
    )
```

```python
import math

import jax
import jax.numpy as jnp
from jax import lax
from jax.experimental import pallas as pl
from jax.experimental.pallas import tpu as pltpu
from jax.sharding import PartitionSpec as P

D = 8192
HD = 128
STEPS = 4
GQA = 8
REQUESTS = 8
SOURCES = 128
PIECE = 64
TP = 8
CTX = 16
HEAD_ROWS = STEPS * GQA

ROPE_BASE = 500000.0
ROPE_FACTOR = 8.0
LOW_FACTOR = 1.0
HIGH_FACTOR = 4.0
ROPE_ANCHOR = 8192.0
NEGATIVE = -1e30
SCALE = HD ** (-0.5)


def angles(positions, width):
    base_freq = ROPE_BASE ** (-(2.0 * jnp.arange(width // 2, dtype=jnp.float32)) / width)
    wavelength = 2.0 * math.pi / base_freq
    blend = (ROPE_ANCHOR / wavelength - LOW_FACTOR) / (HIGH_FACTOR - LOW_FACTOR)
    middle = (1.0 - blend) * base_freq / ROPE_FACTOR + blend * base_freq
    freq = jnp.where(
        wavelength > ROPE_ANCHOR / LOW_FACTOR,
        base_freq / ROPE_FACTOR,
        jnp.where(wavelength < ROPE_ANCHOR / HIGH_FACTOR, base_freq, middle),
    )
    return positions.astype(jnp.float32)[..., None] * freq


COLUMNS = (GQA + 2) * HD
SIDE = 4


def partial_kernel(x_ref, hidden_ref, gain_ref, w_ref, *out_refs):
    rows = STEPS * REQUESTS
    share = rows // SIDE
    target = lax.broadcasted_iota(jnp.int32, (rows, rows), 0)
    origin = lax.broadcasted_iota(jnp.int32, (rows, rows), 1)
    receiver = jnp.bitwise_xor(target // share, x_ref[0])
    request = receiver * (REQUESTS // SIDE) + target % share // STEPS
    moves = jnp.where(origin == target % STEPS * REQUESTS + request, 1.0, 0.0)
    values = jnp.dot(
        moves.astype(jnp.bfloat16), hidden_ref[...], preferred_element_type=jnp.float32
    )
    square = jnp.sum(values * values, axis=1, keepdims=True)
    gain = gain_ref[...].astype(jnp.float32).reshape(1, -1)
    scaled = (values * gain).astype(jnp.bfloat16)
    proj = jnp.dot(scaled, w_ref[...], preferred_element_type=jnp.float32)
    square = jnp.broadcast_to(square, (rows, HD))
    for index, out_ref in enumerate(out_refs):
        out_ref[:, pl.ds(0, COLUMNS)] = proj[index * share:(index + 1) * share]
        out_ref[:, pl.ds(COLUMNS, HD)] = square[index * share:(index + 1) * share]


def partial_projection(x, hidden_states, norm_gain, w_qkv):
    vmem = pl.BlockSpec(memory_space=pltpu.VMEM)
    shape = jax.ShapeDtypeStruct((STEPS * REQUESTS // SIDE, COLUMNS + HD), jnp.float32)
    return pl.pallas_call(
        partial_kernel,
        in_specs=[pl.BlockSpec(memory_space=pltpu.SMEM), vmem, vmem, vmem],
        out_specs=[vmem] * SIDE,
        out_shape=[shape] * SIDE,
        compiler_params=pltpu.CompilerParams(vmem_limit_bytes=8 * 1024 * 1024),
        name="partial_projection",
    )(x.reshape(1), hidden_states, norm_gain, w_qkv)


def swap(value, axis, other):
    pairs = [(index, index ^ other) for index in range(lax.axis_size(axis))]
    return lax.ppermute(value, axis, pairs)


GROUP = 2


def prep_kernel(kv_ref, out_ref, held, ready, in_sems, out_sems):
    def fetch(index):
        span = pl.ds(index * GROUP, GROUP)
        return pltpu.make_async_copy(kv_ref.at[span], held.at[span], in_sems.at[index])

    def place(index):
        span = pl.ds(index * GROUP, GROUP)
        return pltpu.make_async_copy(ready.at[span], out_ref.at[span], out_sems.at[index])

    for index in range(CTX // GROUP):
        fetch(index).start()
    for index in range(CTX // GROUP):
        fetch(index).wait()
        for receiver in range(index * GROUP, (index + 1) * GROUP):
            for head in range(TP):
                ready[receiver, head] = held[receiver, :, :, pl.ds(head * HD, HD)]
        place(index).start()
    for index in range(CTX // GROUP):
        place(index).wait()


def prep(kv_cache):
    split = kv_cache.reshape(CTX, PIECE, 2, TP * HD)
    return pl.pallas_call(
        prep_kernel,
        out_shape=jax.ShapeDtypeStruct((CTX, TP, PIECE, 2, HD), jnp.bfloat16),
        in_specs=[pl.BlockSpec(memory_space=pl.ANY)],
        out_specs=pl.BlockSpec(memory_space=pl.ANY),
        scratch_shapes=[
            pltpu.VMEM((CTX, PIECE, 2, TP * HD), jnp.bfloat16),
            pltpu.VMEM((CTX, TP, PIECE, 2, HD), jnp.bfloat16),
            pltpu.SemaphoreType.DMA((CTX // GROUP,)),
            pltpu.SemaphoreType.DMA((CTX // GROUP,)),
        ],
        compiler_params=pltpu.CompilerParams(vmem_limit_bytes=56 * 1024 * 1024),
        cost_estimate=pl.CostEstimate(
            flops=0, transcendentals=0, bytes_accessed=4 * kv_cache.size
        ),
        name="cache_by_receiver",
    )(split)


CHUNKS = 4
CHUNK_CTX = CTX // CHUNKS
CHUNK_SOURCES = SOURCES // CHUNKS
CHUNK_KEYS = CHUNK_SOURCES * PIECE
CHUNK_ROWS = CHUNK_KEYS * 2
STATE_ROWS = HEAD_ROWS + 16


EARLY = CTX // GROUP // 2


def copy_kernel(kv_ref, out_ref, held, in_sems, out_sems):
    def fetch(index):
        span = pl.ds(index * GROUP, GROUP)
        return pltpu.make_async_copy(kv_ref.at[span], held.at[span], in_sems.at[index])

    def place(index):
        span = pl.ds(index * GROUP, GROUP)
        return pltpu.make_async_copy(held.at[span], out_ref.at[span], out_sems.at[index])

    for index in range(EARLY):
        fetch(index).start()
    for index in range(EARLY):
        fetch(index).wait()
        place(index).start()
    for index in range(EARLY):
        place(index).wait()


def copy_first(moved):
    anywhere = pl.BlockSpec(memory_space=pl.ANY)
    return pl.pallas_call(
        copy_kernel,
        in_specs=[anywhere],
        out_specs=anywhere,
        scratch_shapes=[
            pltpu.VMEM((EARLY * GROUP,) + moved.shape[1:], moved.dtype),
            pltpu.SemaphoreType.DMA((EARLY,)),
            pltpu.SemaphoreType.DMA((EARLY,)),
        ],
        out_shape=jax.ShapeDtypeStruct(moved.shape, moved.dtype),
        compiler_params=pltpu.CompilerParams(vmem_limit_bytes=56 * 1024 * 1024),
        cost_estimate=pl.CostEstimate(
            flops=0, transcendentals=0, bytes_accessed=2 * moved.size
        ),
        name="copy_first",
    )(moved)


def attend_kernel(
    info_ref, kv_ref, own_ref, first_ref, second_ref, third_ref, cos_ref, sin_ref, part_ref,
    kv_out_ref, out_ref,
    held, wide, pairs, query, scores, peaks, top, total, acc, in_sems, out_sems,
):
    del part_ref
    length = info_ref[0]
    part = info_ref[1]
    left = length - part * PIECE

    def fetch(index):
        span = pl.ds(index * GROUP, GROUP)
        return pltpu.make_async_copy(kv_ref.at[span], held.at[span], in_sems.at[index])

    def place(index):
        span = pl.ds(index * GROUP, GROUP)
        return pltpu.make_async_copy(held.at[span], kv_out_ref.at[span], out_sems.at[index])

    for index in range(CTX // GROUP):
        fetch(index).start()

    row = lax.broadcasted_iota(jnp.int32, (HEAD_ROWS, HD), 0)
    lane = lax.broadcasted_iota(jnp.int32, (HEAD_ROWS, HD), 1)
    slot = lane // PIECE * (2 * PIECE) + lane % PIECE

    summed = own_ref[...] + first_ref[...] + second_ref[...] + third_ref[...]
    norm = lax.rsqrt(summed[:, COLUMNS:] / D + 1e-05)

    def head(index):
        return summed[:, index * HD:(index + 1) * HD] * norm

    def turn(vec):
        return vec * cos_ref[...] + pltpu.roll(vec, HD // 2, 1) * sin_ref[...]

    query[...] = jnp.concatenate([turn(head(g)) for g in range(GQA)], axis=0).astype(jnp.bfloat16)
    rest = jnp.zeros((HD - STEPS, HD), jnp.float32)
    keys = jnp.concatenate([turn(head(GQA)), rest], axis=0).astype(jnp.bfloat16)
    values = jnp.concatenate([head(GQA + 1), rest], axis=0).astype(jnp.bfloat16)
    fresh = lax.dot_general(
        query[...], keys, (((1,), (1,)), ((), ())), preferred_element_type=jnp.float32
    ) * SCALE
    live = jnp.logical_and(lane <= row % STEPS, part == 0)
    fresh = jnp.where(live, fresh, NEGATIVE)
    high = jnp.max(fresh, axis=1, keepdims=True)
    weight = jnp.where(live, jnp.exp(fresh - high), 0.0)
    top[...] = jnp.broadcast_to(high, (HEAD_ROWS, HD))
    total[...] = weight
    acc[...] = jnp.dot(weight.astype(jnp.bfloat16), values, preferred_element_type=jnp.float32)

    def arrive(chunk):
        for index in range(chunk * CHUNK_CTX // GROUP, (chunk + 1) * CHUNK_CTX // GROUP):
            fetch(index).wait()
            if index >= EARLY:
                place(index).start()

    def score(chunk):
        wide[...] = held[pl.ds(chunk * CHUNK_CTX, CHUNK_CTX)].reshape(CHUNK_ROWS, HD).astype(
            jnp.float32
        )
        for index in range(2):
            pairs[chunk % 2, index] = wide[pl.ds(index, CHUNK_KEYS, stride=2), :].astype(
                jnp.bfloat16
            )
        found = lax.dot_general(
            query[...],
            pairs[chunk % 2, 0],
            (((1,), (1,)), ((), ())),
            preferred_element_type=jnp.float32,
        )
        peak = None
        for index in range(CHUNK_KEYS // HD):
            source = chunk * CHUNK_SOURCES + index * 2
            piece = found[:, index * HD:(index + 1) * HD] * SCALE
            piece = jnp.where(slot < left - source * (2 * PIECE), piece, NEGATIVE)
            scores[chunk % 2, :, pl.ds(index * HD, HD)] = piece
            peak = piece if peak is None else jnp.maximum(peak, piece)
        peaks[chunk % 2] = peak

    def fold(chunk):
        high = jnp.maximum(top[...], jnp.max(peaks[chunk % 2], axis=1, keepdims=True))
        fade = jnp.exp(top[...] - high)
        summed = total[...] * fade
        pieces = []
        for index in range(CHUNK_KEYS // HD):
            weight = jnp.exp(scores[chunk % 2, :, pl.ds(index * HD, HD)] - high)
            summed = summed + weight
            pieces.append(weight.astype(jnp.bfloat16))
        top[...] = high
        total[...] = summed
        acc[...] = acc[...] * fade + jnp.dot(
            jnp.concatenate(pieces, axis=1),
            pairs[chunk % 2, 1],
            preferred_element_type=jnp.float32,
        )

    arrive(0)

    @pl.when(left > 0)
    def _():
        score(0)

    for chunk in range(CHUNKS):
        if chunk + 1 < CHUNKS:
            arrive(chunk + 1)

        @pl.when(chunk * CHUNK_SOURCES * 2 * PIECE < left)
        def _(chunk=chunk):
            if chunk + 1 < CHUNKS:
                score(chunk + 1)
            fold(chunk)

    count = jnp.sum(total[...], axis=1, keepdims=True)
    some = count > 0.0
    safe = jnp.where(some, count, 1.0)
    out_ref[pl.ds(0, HEAD_ROWS), :] = (acc[...] / safe).astype(jnp.bfloat16)
    level = jnp.where(some, top[...] + jnp.log(safe), NEGATIVE)
    level = jnp.sum(jnp.where(row == lane, level, 0.0), axis=0, keepdims=True)
    first = level.astype(jnp.bfloat16).astype(jnp.float32)
    second = (level - first).astype(jnp.bfloat16).astype(jnp.float32)
    third = level - first - second
    place_in = lax.broadcasted_iota(jnp.int32, (16, HD), 0)
    parts = jnp.where(place_in == 0, first, jnp.where(place_in == 1, second, third))
    out_ref[pl.ds(HEAD_ROWS, 16), :] = parts.astype(jnp.bfloat16)

    for index in range(EARLY, CTX // GROUP):
        place(index).wait()


def attend(info, moved, sums, cosine, sine, copied):
    anywhere = pl.BlockSpec(memory_space=pl.ANY)
    vmem = pl.BlockSpec(memory_space=pltpu.VMEM)
    return pl.pallas_call(
        attend_kernel,
        in_specs=[pl.BlockSpec(memory_space=pltpu.SMEM), anywhere] + [vmem] * 6 + [anywhere],
        input_output_aliases={8: 0},
        out_specs=[anywhere, vmem],
        scratch_shapes=[
            pltpu.VMEM((CTX, TP, 2 * PIECE, HD), jnp.bfloat16),
            pltpu.VMEM((CHUNK_ROWS, HD), jnp.float32),
            pltpu.VMEM((2, 2, CHUNK_KEYS, HD), jnp.bfloat16),
            pltpu.VMEM((HEAD_ROWS, HD), jnp.bfloat16),
            pltpu.VMEM((2, HEAD_ROWS, CHUNK_KEYS), jnp.float32),
            pltpu.VMEM((2, HEAD_ROWS, HD), jnp.float32),
            pltpu.VMEM((HEAD_ROWS, HD), jnp.float32),
            pltpu.VMEM((HEAD_ROWS, HD), jnp.float32),
            pltpu.VMEM((HEAD_ROWS, HD), jnp.float32),
            pltpu.SemaphoreType.DMA((CTX // GROUP,)),
            pltpu.SemaphoreType.DMA((CTX // GROUP,)),
        ],
        out_shape=[
            jax.ShapeDtypeStruct((CTX, TP, 2 * PIECE, HD), jnp.bfloat16),
            jax.ShapeDtypeStruct((STATE_ROWS, HD), jnp.bfloat16),
        ],
        compiler_params=pltpu.CompilerParams(vmem_limit_bytes=24 * 1024 * 1024),
        name="attend",
    )(info, moved, *sums, cosine, sine, copied)


def project_kernel(states_ref, w_ref, *refs):
    base_ref, out_ref = refs if len(refs) == 2 else (None, refs[0])
    row = lax.broadcasted_iota(jnp.int32, (HEAD_ROWS, HD), 0)
    lane = lax.broadcasted_iota(jnp.int32, (HEAD_ROWS, HD), 1)
    many = REQUESTS * HEAD_ROWS
    target = lax.broadcasted_iota(jnp.int32, (many, many), 0)
    origin = lax.broadcasted_iota(jnp.int32, (many, many), 1)
    head = target // (STEPS * REQUESTS)
    step = target // REQUESTS % STEPS
    request = target % REQUESTS
    moves = jnp.where(origin == request * HEAD_ROWS + head * STEPS + step, 1.0, 0.0)
    rows = []
    for request in range(REQUESTS):
        spots = [2 * request + part for part in range(2)]
        levels = []
        for spot in spots:
            coded = states_ref[spot, pl.ds(HEAD_ROWS, 16), :].astype(jnp.float32)
            level = coded[0:1] + coded[1:2] + coded[2:3]
            levels.append(jnp.sum(jnp.where(row == lane, level, 0.0), axis=1, keepdims=True))
        high = jnp.maximum(levels[0], levels[1])
        shares = [jnp.exp(level - high) for level in levels]
        whole = shares[0] + shares[1]
        mixed = sum(
            states_ref[spot, pl.ds(0, HEAD_ROWS), :].astype(jnp.float32) * (share / whole)
            for spot, share in zip(spots, shares)
        )
        rows.append(mixed.astype(jnp.bfloat16))
    attn = jnp.dot(
        moves.astype(jnp.bfloat16),
        jnp.concatenate(rows, axis=0),
        preferred_element_type=jnp.float32,
    ).astype(jnp.bfloat16)
    total = jnp.zeros(out_ref.shape, jnp.float32)
    for index in range(GQA):
        total = total + jnp.dot(
            attn[index * HEAD_ROWS:(index + 1) * HEAD_ROWS],
            w_ref[pl.ds(index * HD, HD), :],
            preferred_element_type=jnp.float32,
        )
    if base_ref is not None:
        total = total + base_ref[...]
    out_ref[...] = total.astype(out_ref.dtype)


def project(states, w, base=None):
    vmem = pl.BlockSpec(memory_space=pltpu.VMEM)
    operands = (states, w) if base is None else (states, w, base)
    kind = jnp.float32 if base is None else jnp.bfloat16
    return pl.pallas_call(
        project_kernel,
        in_specs=[vmem] * len(operands),
        out_specs=vmem,
        out_shape=jax.ShapeDtypeStruct((STEPS * REQUESTS, w.shape[1]), kind),
        compiler_params=pltpu.CompilerParams(vmem_limit_bytes=8 * 1024 * 1024),
        name="project",
    )(*operands)


def per_device(hidden_states, norm_gain, prompt_lengths, kv_cache, w_qkv, w_out):
    x = lax.axis_index("x")
    y = lax.axis_index("y")
    mine = x * (REQUESTS // SIDE) + y // 2
    part = y % 2
    length = lax.dynamic_index_in_dim(prompt_lengths, mine, 0, keepdims=False)

    ready = prep(kv_cache).reshape(CTX * TP, 2 * PIECE, HD)
    everyone = ("x", "y", "z", "core")
    moved = lax.all_to_all(ready, everyone, split_axis=0, concat_axis=0, tiled=True)
    moved = moved.reshape(CTX, TP, 2 * PIECE, HD)

    _, hidden_states = lax.optimization_barrier((ready, hidden_states))
    packed = partial_projection(x, hidden_states, norm_gain, w_qkv)
    packed, w_out = lax.optimization_barrier((packed, w_out))
    along_x = packed[0] + sum(swap(packed[k], "x", k) for k in range(1, SIDE))
    w_mate = swap(w_out, "core", 1)
    along_x = along_x.reshape(2, STEPS, COLUMNS + HD)
    own = lax.dynamic_index_in_dim(along_x, y // 2, 0, keepdims=False)
    far = lax.dynamic_index_in_dim(along_x, 1 - y // 2, 0, keepdims=False)
    sums = [own, swap(own, "y", 1), swap(far, "y", 3), swap(far, "y", 2)]

    angle = angles(length + jnp.arange(STEPS, dtype=jnp.int32), HD)
    cosine = jnp.cos(angle)
    sine = jnp.sin(angle)
    cosine = jnp.concatenate([cosine, cosine], axis=1)
    sine = jnp.concatenate([-sine, sine], axis=1)
    info = jnp.stack([length, part]).astype(jnp.int32)
    kv_decode, state = attend(info, moved, sums, cosine, sine, copy_first(moved))
    kv_decode = kv_decode.reshape(1, SOURCES, PIECE, 2, HD)

    states = jnp.broadcast_to(state[None], (CTX, STATE_ROWS, HD))
    states = lax.all_to_all(states, ("x", "y"), split_axis=0, concat_axis=0, tiled=True)
    mate_states = swap(states, "core", 1)
    out = project(mate_states, w_mate, project(states, w_out))
    pairs = [(z * 2 + c, (z ^ (1 + 2 * c)) * 2 + c) for z in range(SIDE) for c in range(2)]
    near = lax.ppermute(out, ("z", "core"), pairs)
    across = swap(out, "z", 2)
    shared = swap(near, "core", 1)
    first = lax.axis_index("core") == 0
    one = jnp.where(first, near, shared).astype(jnp.float32)
    three = jnp.where(first, shared, near).astype(jnp.float32)
    block_out = (out.astype(jnp.float32) + one) + (across.astype(jnp.float32) + three)
    block_out = block_out.astype(jnp.bfloat16)
    return (block_out, kv_decode)


def solution(mesh):
    fine = jax.sharding.Mesh(
        mesh.devices.reshape(SIDE, SIDE, SIDE, 2), ("x", "y", "z", "core")
    )
    ctx, tp = ("x", "y"), ("z", "core")
    return jax.shard_map(
        per_device,
        mesh=fine,
        in_specs=(
            P(None, ctx),
            P(ctx),
            P(),
            P(None, ctx + tp, None, None),
            P(ctx, tp),
            P(tp, ctx),
        ),
        out_specs=(P(None, ctx), P(ctx, None, None, None, tp)),
        check_vma=False,
    )
```

```python
import math

import jax
import jax.numpy as jnp
from jax import lax
from jax.experimental import pallas as pl
from jax.experimental.pallas import tpu as pltpu
from jax.sharding import PartitionSpec as P

D = 8192
HD = 128
STEPS = 4
GQA = 8
REQUESTS = 8
SOURCES = 128
PIECE = 64
TP = 8
CTX = 16
HEAD_ROWS = STEPS * GQA

ROPE_BASE = 500000.0
ROPE_FACTOR = 8.0
LOW_FACTOR = 1.0
HIGH_FACTOR = 4.0
ROPE_ANCHOR = 8192.0
NEGATIVE = -1e30
SCALE = HD ** (-0.5)


def angles(positions, width):
    base_freq = ROPE_BASE ** (-(2.0 * jnp.arange(width // 2, dtype=jnp.float32)) / width)
    wavelength = 2.0 * math.pi / base_freq
    blend = (ROPE_ANCHOR / wavelength - LOW_FACTOR) / (HIGH_FACTOR - LOW_FACTOR)
    middle = (1.0 - blend) * base_freq / ROPE_FACTOR + blend * base_freq
    freq = jnp.where(
        wavelength > ROPE_ANCHOR / LOW_FACTOR,
        base_freq / ROPE_FACTOR,
        jnp.where(wavelength < ROPE_ANCHOR / HIGH_FACTOR, base_freq, middle),
    )
    return positions.astype(jnp.float32)[..., None] * freq


COLUMNS = (GQA + 2) * HD
SIDE = 4


def partial_kernel(x_ref, hidden_ref, gain_ref, w_ref, *out_refs):
    rows = STEPS * REQUESTS
    share = rows // SIDE
    target = lax.broadcasted_iota(jnp.int32, (rows, rows), 0)
    origin = lax.broadcasted_iota(jnp.int32, (rows, rows), 1)
    receiver = jnp.bitwise_xor(target // share, x_ref[0])
    request = receiver * (REQUESTS // SIDE) + target % share // STEPS
    moves = jnp.where(origin == target % STEPS * REQUESTS + request, 1.0, 0.0)
    values = jnp.dot(
        moves.astype(jnp.bfloat16), hidden_ref[...], preferred_element_type=jnp.float32
    )
    square = jnp.sum(values * values, axis=1, keepdims=True)
    gain = gain_ref[...].astype(jnp.float32).reshape(1, -1)
    scaled = (values * gain).astype(jnp.bfloat16)
    proj = jnp.dot(scaled, w_ref[...], preferred_element_type=jnp.float32)
    square = jnp.broadcast_to(square, (rows, HD))
    first = square.astype(jnp.bfloat16).astype(jnp.float32)
    second = (square - first).astype(jnp.bfloat16).astype(jnp.float32)
    terms = (first, second, square - first - second)
    for index, out_ref in enumerate(out_refs):
        span = slice(index * share, (index + 1) * share)
        out_ref[:, pl.ds(0, COLUMNS)] = proj[span].astype(jnp.bfloat16)
        for spot, term in enumerate(terms):
            out_ref[:, pl.ds(COLUMNS + spot * HD, HD)] = term[span].astype(jnp.bfloat16)


def partial_projection(x, hidden_states, norm_gain, w_qkv):
    vmem = pl.BlockSpec(memory_space=pltpu.VMEM)
    shape = jax.ShapeDtypeStruct((STEPS * REQUESTS // SIDE, COLUMNS + 3 * HD), jnp.bfloat16)
    return pl.pallas_call(
        partial_kernel,
        in_specs=[pl.BlockSpec(memory_space=pltpu.SMEM), vmem, vmem, vmem],
        out_specs=[vmem] * SIDE,
        out_shape=[shape] * SIDE,
        compiler_params=pltpu.CompilerParams(vmem_limit_bytes=8 * 1024 * 1024),
        name="partial_projection",
    )(x.reshape(1), hidden_states, norm_gain, w_qkv)


def swap(value, axis, other):
    pairs = [(index, index ^ other) for index in range(lax.axis_size(axis))]
    return lax.ppermute(value, axis, pairs)


GROUP = 2


def prep_kernel(kv_ref, out_ref, held, ready, in_sems, out_sems):
    def fetch(index):
        span = pl.ds(index * GROUP, GROUP)
        return pltpu.make_async_copy(kv_ref.at[span], held.at[span], in_sems.at[index])

    def place(index):
        span = pl.ds(index * GROUP, GROUP)
        return pltpu.make_async_copy(ready.at[span], out_ref.at[span], out_sems.at[index])

    for index in range(CTX // GROUP):
        fetch(index).start()
    for index in range(CTX // GROUP):
        fetch(index).wait()
        for receiver in range(index * GROUP, (index + 1) * GROUP):
            for head in range(TP):
                ready[receiver, head] = held[receiver, :, :, pl.ds(head * HD, HD)]
        place(index).start()
    for index in range(CTX // GROUP):
        place(index).wait()


def prep(kv_cache):
    split = kv_cache.reshape(CTX, PIECE, 2, TP * HD)
    return pl.pallas_call(
        prep_kernel,
        out_shape=jax.ShapeDtypeStruct((CTX, TP, PIECE, 2, HD), jnp.bfloat16),
        in_specs=[pl.BlockSpec(memory_space=pl.ANY)],
        out_specs=pl.BlockSpec(memory_space=pl.ANY),
        scratch_shapes=[
            pltpu.VMEM((CTX, PIECE, 2, TP * HD), jnp.bfloat16),
            pltpu.VMEM((CTX, TP, PIECE, 2, HD), jnp.bfloat16),
            pltpu.SemaphoreType.DMA((CTX // GROUP,)),
            pltpu.SemaphoreType.DMA((CTX // GROUP,)),
        ],
        compiler_params=pltpu.CompilerParams(vmem_limit_bytes=56 * 1024 * 1024),
        cost_estimate=pl.CostEstimate(
            flops=0, transcendentals=0, bytes_accessed=4 * kv_cache.size
        ),
        name="cache_by_receiver",
    )(split)


CHUNKS = 4
CHUNK_CTX = CTX // CHUNKS
CHUNK_SOURCES = SOURCES // CHUNKS
CHUNK_KEYS = CHUNK_SOURCES * PIECE
CHUNK_ROWS = CHUNK_KEYS * 2
STATE_ROWS = HEAD_ROWS + 16


def attend_kernel(
    info_ref, kv_ref, own_ref, first_ref, second_ref, third_ref, cos_ref, sin_ref,
    kv_out_ref, out_ref,
    held, wide, pairs, query, scores, peaks, top, total, acc, in_sems, out_sems,
):
    length = info_ref[0]
    part = info_ref[1]
    left = length - part * PIECE

    def fetch(index):
        span = pl.ds(index * GROUP, GROUP)
        return pltpu.make_async_copy(kv_ref.at[span], held.at[span], in_sems.at[index])

    def place(index):
        span = pl.ds(index * GROUP, GROUP)
        return pltpu.make_async_copy(held.at[span], kv_out_ref.at[span], out_sems.at[index])

    for index in range(CTX // GROUP):
        fetch(index).start()

    row = lax.broadcasted_iota(jnp.int32, (HEAD_ROWS, HD), 0)
    lane = lax.broadcasted_iota(jnp.int32, (HEAD_ROWS, HD), 1)
    slot = lane // PIECE * (2 * PIECE) + lane % PIECE

    summed = own_ref[...] + first_ref[...] + second_ref[...] + third_ref[...]
    norm = lax.rsqrt(summed[:, COLUMNS:] / D + 1e-05)

    def head(index):
        return summed[:, index * HD:(index + 1) * HD] * norm

    def turn(vec):
        return vec * cos_ref[...] + pltpu.roll(vec, HD // 2, 1) * sin_ref[...]

    query[...] = jnp.concatenate([turn(head(g)) for g in range(GQA)], axis=0).astype(jnp.bfloat16)
    rest = jnp.zeros((HD - STEPS, HD), jnp.float32)
    keys = jnp.concatenate([turn(head(GQA)), rest], axis=0).astype(jnp.bfloat16)
    values = jnp.concatenate([head(GQA + 1), rest], axis=0).astype(jnp.bfloat16)
    fresh = lax.dot_general(
        query[...], keys, (((1,), (1,)), ((), ())), preferred_element_type=jnp.float32
    ) * SCALE
    live = jnp.logical_and(lane <= row % STEPS, part == 0)
    fresh = jnp.where(live, fresh, NEGATIVE)
    high = jnp.max(fresh, axis=1, keepdims=True)
    weight = jnp.where(live, jnp.exp(fresh - high), 0.0)
    top[...] = jnp.broadcast_to(high, (HEAD_ROWS, HD))
    total[...] = weight
    acc[...] = jnp.dot(weight.astype(jnp.bfloat16), values, preferred_element_type=jnp.float32)

    def arrive(chunk):
        for index in range(chunk * CHUNK_CTX // GROUP, (chunk + 1) * CHUNK_CTX // GROUP):
            fetch(index).wait()
            place(index).start()

    def score(chunk):
        wide[...] = held[pl.ds(chunk * CHUNK_CTX, CHUNK_CTX)].reshape(CHUNK_ROWS, HD).astype(
            jnp.float32
        )
        for index in range(2):
            pairs[chunk % 2, index] = wide[pl.ds(index, CHUNK_KEYS, stride=2), :].astype(
                jnp.bfloat16
            )
        found = lax.dot_general(
            query[...],
            pairs[chunk % 2, 0],
            (((1,), (1,)), ((), ())),
            preferred_element_type=jnp.float32,
        )
        peak = None
        for index in range(CHUNK_KEYS // HD):
            source = chunk * CHUNK_SOURCES + index * 2
            piece = found[:, index * HD:(index + 1) * HD] * SCALE
            piece = jnp.where(slot < left - source * (2 * PIECE), piece, NEGATIVE)
            scores[chunk % 2, :, pl.ds(index * HD, HD)] = piece
            peak = piece if peak is None else jnp.maximum(peak, piece)
        peaks[chunk % 2] = peak

    def fold(chunk):
        high = jnp.maximum(top[...], jnp.max(peaks[chunk % 2], axis=1, keepdims=True))
        fade = jnp.exp(top[...] - high)
        summed = total[...] * fade
        pieces = []
        for index in range(CHUNK_KEYS // HD):
            weight = jnp.exp(scores[chunk % 2, :, pl.ds(index * HD, HD)] - high)
            summed = summed + weight
            pieces.append(weight.astype(jnp.bfloat16))
        top[...] = high
        total[...] = summed
        acc[...] = acc[...] * fade + jnp.dot(
            jnp.concatenate(pieces, axis=1),
            pairs[chunk % 2, 1],
            preferred_element_type=jnp.float32,
        )

    arrive(0)

    @pl.when(left > 0)
    def _():
        score(0)

    for chunk in range(CHUNKS):
        if chunk + 1 < CHUNKS:
            arrive(chunk + 1)

        @pl.when(chunk * CHUNK_SOURCES * 2 * PIECE < left)
        def _(chunk=chunk):
            if chunk + 1 < CHUNKS:
                score(chunk + 1)
            fold(chunk)

    count = jnp.sum(total[...], axis=1, keepdims=True)
    some = count > 0.0
    safe = jnp.where(some, count, 1.0)
    out_ref[pl.ds(0, HEAD_ROWS), :] = (acc[...] / safe).astype(jnp.bfloat16)
    level = jnp.where(some, top[...] + jnp.log(safe), NEGATIVE)
    level = jnp.sum(jnp.where(row == lane, level, 0.0), axis=0, keepdims=True)
    first = level.astype(jnp.bfloat16).astype(jnp.float32)
    second = (level - first).astype(jnp.bfloat16).astype(jnp.float32)
    third = level - first - second
    place_in = lax.broadcasted_iota(jnp.int32, (16, HD), 0)
    parts = jnp.where(place_in == 0, first, jnp.where(place_in == 1, second, third))
    out_ref[pl.ds(HEAD_ROWS, 16), :] = parts.astype(jnp.bfloat16)

    for index in range(CTX // GROUP):
        place(index).wait()


def attend(info, moved, sums, cosine, sine):
    anywhere = pl.BlockSpec(memory_space=pl.ANY)
    vmem = pl.BlockSpec(memory_space=pltpu.VMEM)
    return pl.pallas_call(
        attend_kernel,
        in_specs=[pl.BlockSpec(memory_space=pltpu.SMEM), anywhere] + [vmem] * 6,
        out_specs=[anywhere, vmem],
        scratch_shapes=[
            pltpu.VMEM((CTX, TP, 2 * PIECE, HD), jnp.bfloat16),
            pltpu.VMEM((CHUNK_ROWS, HD), jnp.float32),
            pltpu.VMEM((2, 2, CHUNK_KEYS, HD), jnp.bfloat16),
            pltpu.VMEM((HEAD_ROWS, HD), jnp.bfloat16),
            pltpu.VMEM((2, HEAD_ROWS, CHUNK_KEYS), jnp.float32),
            pltpu.VMEM((2, HEAD_ROWS, HD), jnp.float32),
            pltpu.VMEM((HEAD_ROWS, HD), jnp.float32),
            pltpu.VMEM((HEAD_ROWS, HD), jnp.float32),
            pltpu.VMEM((HEAD_ROWS, HD), jnp.float32),
            pltpu.SemaphoreType.DMA((CTX // GROUP,)),
            pltpu.SemaphoreType.DMA((CTX // GROUP,)),
        ],
        out_shape=[
            jax.ShapeDtypeStruct((CTX, TP, 2 * PIECE, HD), jnp.bfloat16),
            jax.ShapeDtypeStruct((STATE_ROWS, HD), jnp.bfloat16),
        ],
        compiler_params=pltpu.CompilerParams(vmem_limit_bytes=24 * 1024 * 1024),
        name="attend",
    )(info, moved, *sums, cosine, sine)


def project_kernel(states_ref, w_ref, *refs):
    base_ref, out_ref = refs if len(refs) == 2 else (None, refs[0])
    row = lax.broadcasted_iota(jnp.int32, (HEAD_ROWS, HD), 0)
    lane = lax.broadcasted_iota(jnp.int32, (HEAD_ROWS, HD), 1)
    many = REQUESTS * HEAD_ROWS
    target = lax.broadcasted_iota(jnp.int32, (many, many), 0)
    origin = lax.broadcasted_iota(jnp.int32, (many, many), 1)
    head = target // (STEPS * REQUESTS)
    step = target // REQUESTS % STEPS
    request = target % REQUESTS
    moves = jnp.where(origin == request * HEAD_ROWS + head * STEPS + step, 1.0, 0.0)
    rows = []
    for request in range(REQUESTS):
        spots = [2 * request + part for part in range(2)]
        levels = []
        for spot in spots:
            coded = states_ref[spot, pl.ds(HEAD_ROWS, 16), :].astype(jnp.float32)
            level = coded[0:1] + coded[1:2] + coded[2:3]
            levels.append(jnp.sum(jnp.where(row == lane, level, 0.0), axis=1, keepdims=True))
        high = jnp.maximum(levels[0], levels[1])
        shares = [jnp.exp(level - high) for level in levels]
        whole = shares[0] + shares[1]
        mixed = sum(
            states_ref[spot, pl.ds(0, HEAD_ROWS), :].astype(jnp.float32) * (share / whole)
            for spot, share in zip(spots, shares)
        )
        rows.append(mixed.astype(jnp.bfloat16))
    attn = jnp.dot(
        moves.astype(jnp.bfloat16),
        jnp.concatenate(rows, axis=0),
        preferred_element_type=jnp.float32,
    ).astype(jnp.bfloat16)
    total = jnp.zeros(out_ref.shape, jnp.float32)
    for index in range(GQA):
        total = total + jnp.dot(
            attn[index * HEAD_ROWS:(index + 1) * HEAD_ROWS],
            w_ref[pl.ds(index * HD, HD), :],
            preferred_element_type=jnp.float32,
        )
    if base_ref is not None:
        total = total + base_ref[...]
    out_ref[...] = total.astype(out_ref.dtype)


def project(states, w, base=None):
    vmem = pl.BlockSpec(memory_space=pltpu.VMEM)
    operands = (states, w) if base is None else (states, w, base)
    kind = jnp.float32 if base is None else jnp.bfloat16
    return pl.pallas_call(
        project_kernel,
        in_specs=[vmem] * len(operands),
        out_specs=vmem,
        out_shape=jax.ShapeDtypeStruct((STEPS * REQUESTS, w.shape[1]), kind),
        compiler_params=pltpu.CompilerParams(vmem_limit_bytes=8 * 1024 * 1024),
        name="project",
    )(*operands)


def per_device(hidden_states, norm_gain, prompt_lengths, kv_cache, w_qkv, w_out):
    x = lax.axis_index("x")
    y = lax.axis_index("y")
    mine = x * (REQUESTS // SIDE) + y // 2
    part = y % 2
    length = lax.dynamic_index_in_dim(prompt_lengths, mine, 0, keepdims=False)

    ready = prep(kv_cache).reshape(CTX * TP, 2 * PIECE, HD)
    everyone = ("x", "y", "z", "core")
    moved = lax.all_to_all(ready, everyone, split_axis=0, concat_axis=0, tiled=True)
    moved = moved.reshape(CTX, TP, 2 * PIECE, HD)

    _, hidden_states = lax.optimization_barrier((ready, hidden_states))
    packed = partial_projection(x, hidden_states, norm_gain, w_qkv)
    packed, w_out = lax.optimization_barrier((packed, w_out))
    along_x = sum(
        term.astype(jnp.float32)
        for term in [packed[0]] + [swap(packed[k], "x", k) for k in range(1, SIDE)]
    )
    squares = [along_x[:, COLUMNS + k * HD:COLUMNS + (k + 1) * HD] for k in range(3)]
    along_x = jnp.concatenate([along_x[:, :COLUMNS], sum(squares)], axis=1)
    w_mate = swap(w_out, "core", 1)
    along_x = along_x.reshape(2, STEPS, COLUMNS + HD)
    own = lax.dynamic_index_in_dim(along_x, y // 2, 0, keepdims=False)
    far = lax.dynamic_index_in_dim(along_x, 1 - y // 2, 0, keepdims=False)
    sums = [own, swap(own, "y", 1), swap(far, "y", 3), swap(far, "y", 2)]

    angle = angles(length + jnp.arange(STEPS, dtype=jnp.int32), HD)
    cosine = jnp.cos(angle)
    sine = jnp.sin(angle)
    cosine = jnp.concatenate([cosine, cosine], axis=1)
    sine = jnp.concatenate([-sine, sine], axis=1)
    info = jnp.stack([length, part]).astype(jnp.int32)
    kv_decode, state = attend(info, moved, sums, cosine, sine)
    kv_decode = kv_decode.reshape(1, SOURCES, PIECE, 2, HD)

    states = jnp.broadcast_to(state[None], (CTX, STATE_ROWS, HD))
    states = lax.all_to_all(states, ("x", "y"), split_axis=0, concat_axis=0, tiled=True)
    mate_states = swap(states, "core", 1)
    out = project(mate_states, w_mate, project(states, w_out))
    pairs = [(z * 2 + c, (z ^ (1 + 2 * c)) * 2 + c) for z in range(SIDE) for c in range(2)]
    near = lax.ppermute(out, ("z", "core"), pairs)
    across = swap(out, "z", 2)
    shared = swap(near, "core", 1)
    first = lax.axis_index("core") == 0
    one = jnp.where(first, near, shared).astype(jnp.float32)
    three = jnp.where(first, shared, near).astype(jnp.float32)
    block_out = (out.astype(jnp.float32) + one) + (across.astype(jnp.float32) + three)
    block_out = block_out.astype(jnp.bfloat16)
    return (block_out, kv_decode)


def solution(mesh):
    fine = jax.sharding.Mesh(
        mesh.devices.reshape(SIDE, SIDE, SIDE, 2), ("x", "y", "z", "core")
    )
    ctx, tp = ("x", "y"), ("z", "core")
    return jax.shard_map(
        per_device,
        mesh=fine,
        in_specs=(
            P(None, ctx),
            P(ctx),
            P(),
            P(None, ctx + tp, None, None),
            P(ctx, tp),
            P(tp, ctx),
        ),
        out_specs=(P(None, ctx), P(ctx, None, None, None, tp)),
        check_vma=False,
    )
```

```python
import math

import jax
import jax.numpy as jnp
from jax import lax
from jax.experimental import pallas as pl
from jax.experimental.pallas import tpu as pltpu
from jax.sharding import PartitionSpec as P

D = 8192
HD = 128
STEPS = 4
GQA = 8
REQUESTS = 8
SOURCES = 128
PIECE = 64
TP = 8
CTX = 16
HEAD_ROWS = STEPS * GQA

ROPE_BASE = 500000.0
ROPE_FACTOR = 8.0
LOW_FACTOR = 1.0
HIGH_FACTOR = 4.0
ROPE_ANCHOR = 8192.0
NEGATIVE = -1e30
SCALE = HD ** (-0.5)


def angles(positions, width):
    base_freq = ROPE_BASE ** (-(2.0 * jnp.arange(width // 2, dtype=jnp.float32)) / width)
    wavelength = 2.0 * math.pi / base_freq
    blend = (ROPE_ANCHOR / wavelength - LOW_FACTOR) / (HIGH_FACTOR - LOW_FACTOR)
    middle = (1.0 - blend) * base_freq / ROPE_FACTOR + blend * base_freq
    freq = jnp.where(
        wavelength > ROPE_ANCHOR / LOW_FACTOR,
        base_freq / ROPE_FACTOR,
        jnp.where(wavelength < ROPE_ANCHOR / HIGH_FACTOR, base_freq, middle),
    )
    return positions.astype(jnp.float32)[..., None] * freq


COLUMNS = (GQA + 2) * HD
SIDE = 4


def partial_kernel(x_ref, hidden_ref, gain_ref, w_ref, *out_refs):
    rows = STEPS * REQUESTS
    share = rows // SIDE
    target = lax.broadcasted_iota(jnp.int32, (rows, rows), 0)
    origin = lax.broadcasted_iota(jnp.int32, (rows, rows), 1)
    receiver = jnp.bitwise_xor(target // share, x_ref[0])
    request = receiver * (REQUESTS // SIDE) + target % share // STEPS
    moves = jnp.where(origin == target % STEPS * REQUESTS + request, 1.0, 0.0)
    values = jnp.dot(
        moves.astype(jnp.bfloat16), hidden_ref[...], preferred_element_type=jnp.float32
    )
    square = jnp.sum(values * values, axis=1, keepdims=True)
    gain = gain_ref[...].astype(jnp.float32).reshape(1, -1)
    scaled = (values * gain).astype(jnp.bfloat16)
    proj = jnp.dot(scaled, w_ref[...], preferred_element_type=jnp.float32)
    square = jnp.broadcast_to(square, (rows, HD))
    for index, out_ref in enumerate(out_refs):
        out_ref[:, pl.ds(0, COLUMNS)] = proj[index * share:(index + 1) * share]
        out_ref[:, pl.ds(COLUMNS, HD)] = square[index * share:(index + 1) * share]


def partial_projection(x, hidden_states, norm_gain, w_qkv):
    vmem = pl.BlockSpec(memory_space=pltpu.VMEM)
    shape = jax.ShapeDtypeStruct((STEPS * REQUESTS // SIDE, COLUMNS + HD), jnp.float32)
    return pl.pallas_call(
        partial_kernel,
        in_specs=[pl.BlockSpec(memory_space=pltpu.SMEM), vmem, vmem, vmem],
        out_specs=[vmem] * SIDE,
        out_shape=[shape] * SIDE,
        compiler_params=pltpu.CompilerParams(vmem_limit_bytes=8 * 1024 * 1024),
        name="partial_projection",
    )(x.reshape(1), hidden_states, norm_gain, w_qkv)


def swap(value, axis, other):
    pairs = [(index, index ^ other) for index in range(lax.axis_size(axis))]
    return lax.ppermute(value, axis, pairs)


GROUP = 2


def prep_kernel(kv_ref, out_ref, held, ready, in_sems, out_sems):
    def fetch(index):
        span = pl.ds(index * GROUP, GROUP)
        return pltpu.make_async_copy(kv_ref.at[span], held.at[span], in_sems.at[index])

    def place(index):
        span = pl.ds(index * GROUP, GROUP)
        return pltpu.make_async_copy(ready.at[span], out_ref.at[span], out_sems.at[index])

    for index in range(CTX // GROUP):
        fetch(index).start()
    for index in range(CTX // GROUP):
        fetch(index).wait()
        for receiver in range(index * GROUP, (index + 1) * GROUP):
            for head in range(TP):
                ready[receiver, head] = held[receiver, :, :, pl.ds(head * HD, HD)]
        place(index).start()
    for index in range(CTX // GROUP):
        place(index).wait()


def prep(kv_cache):
    split = kv_cache.reshape(CTX, PIECE, 2, TP * HD)
    return pl.pallas_call(
        prep_kernel,
        out_shape=jax.ShapeDtypeStruct((CTX, TP, PIECE, 2, HD), jnp.bfloat16),
        in_specs=[pl.BlockSpec(memory_space=pl.ANY)],
        out_specs=pl.BlockSpec(memory_space=pl.ANY),
        scratch_shapes=[
            pltpu.VMEM((CTX, PIECE, 2, TP * HD), jnp.bfloat16),
            pltpu.VMEM((CTX, TP, PIECE, 2, HD), jnp.bfloat16),
            pltpu.SemaphoreType.DMA((CTX // GROUP,)),
            pltpu.SemaphoreType.DMA((CTX // GROUP,)),
        ],
        compiler_params=pltpu.CompilerParams(vmem_limit_bytes=56 * 1024 * 1024),
        cost_estimate=pl.CostEstimate(
            flops=0, transcendentals=0, bytes_accessed=4 * kv_cache.size
        ),
        name="cache_by_receiver",
    )(split)


CHUNKS = 2
CHUNK_CTX = CTX // CHUNKS
CHUNK_SOURCES = SOURCES // CHUNKS
CHUNK_KEYS = CHUNK_SOURCES * PIECE
CHUNK_ROWS = CHUNK_KEYS * 2
STATE_ROWS = HEAD_ROWS + 16


def attend_kernel(
    info_ref, kv_ref, own_ref, first_ref, second_ref, third_ref, cos_ref, sin_ref,
    kv_out_ref, out_ref,
    held, wide, pairs, query, scores, peaks, top, total, acc, in_sems, out_sems,
):
    length = info_ref[0]
    part = info_ref[1]
    left = length - part * PIECE

    def fetch(index):
        span = pl.ds(index * GROUP, GROUP)
        return pltpu.make_async_copy(kv_ref.at[span], held.at[span], in_sems.at[index])

    def place(index):
        span = pl.ds(index * GROUP, GROUP)
        return pltpu.make_async_copy(held.at[span], kv_out_ref.at[span], out_sems.at[index])

    for index in range(CTX // GROUP):
        fetch(index).start()

    row = lax.broadcasted_iota(jnp.int32, (HEAD_ROWS, HD), 0)
    lane = lax.broadcasted_iota(jnp.int32, (HEAD_ROWS, HD), 1)
    slot = lane // PIECE * (2 * PIECE) + lane % PIECE

    summed = own_ref[...] + first_ref[...] + second_ref[...] + third_ref[...]
    norm = lax.rsqrt(summed[:, COLUMNS:] / D + 1e-05)

    def head(index):
        return summed[:, index * HD:(index + 1) * HD] * norm

    def turn(vec):
        return vec * cos_ref[...] + pltpu.roll(vec, HD // 2, 1) * sin_ref[...]

    query[...] = jnp.concatenate([turn(head(g)) for g in range(GQA)], axis=0).astype(jnp.bfloat16)
    rest = jnp.zeros((HD - STEPS, HD), jnp.float32)
    keys = jnp.concatenate([turn(head(GQA)), rest], axis=0).astype(jnp.bfloat16)
    values = jnp.concatenate([head(GQA + 1), rest], axis=0).astype(jnp.bfloat16)
    fresh = lax.dot_general(
        query[...], keys, (((1,), (1,)), ((), ())), preferred_element_type=jnp.float32
    ) * SCALE
    live = jnp.logical_and(lane <= row % STEPS, part == 0)
    fresh = jnp.where(live, fresh, NEGATIVE)
    high = jnp.max(fresh, axis=1, keepdims=True)
    weight = jnp.where(live, jnp.exp(fresh - high), 0.0)
    top[...] = jnp.broadcast_to(high, (HEAD_ROWS, HD))
    total[...] = weight
    acc[...] = jnp.dot(weight.astype(jnp.bfloat16), values, preferred_element_type=jnp.float32)

    def arrive(chunk):
        for index in range(chunk * CHUNK_CTX // GROUP, (chunk + 1) * CHUNK_CTX // GROUP):
            fetch(index).wait()
            place(index).start()

    def score(chunk):
        wide[...] = held[pl.ds(chunk * CHUNK_CTX, CHUNK_CTX)].reshape(CHUNK_ROWS, HD).astype(
            jnp.float32
        )
        for index in range(2):
            pairs[chunk % 2, index] = wide[pl.ds(index, CHUNK_KEYS, stride=2), :].astype(
                jnp.bfloat16
            )
        found = lax.dot_general(
            query[...],
            pairs[chunk % 2, 0],
            (((1,), (1,)), ((), ())),
            preferred_element_type=jnp.float32,
        )
        peak = None
        for index in range(CHUNK_KEYS // HD):
            source = chunk * CHUNK_SOURCES + index * 2
            piece = found[:, index * HD:(index + 1) * HD] * SCALE
            piece = jnp.where(slot < left - source * (2 * PIECE), piece, NEGATIVE)
            scores[chunk % 2, :, pl.ds(index * HD, HD)] = piece
            peak = piece if peak is None else jnp.maximum(peak, piece)
        peaks[chunk % 2] = peak

    def fold(chunk):
        high = jnp.maximum(top[...], jnp.max(peaks[chunk % 2], axis=1, keepdims=True))
        fade = jnp.exp(top[...] - high)
        summed = total[...] * fade
        pieces = []
        for index in range(CHUNK_KEYS // HD):
            weight = jnp.exp(scores[chunk % 2, :, pl.ds(index * HD, HD)] - high)
            summed = summed + weight
            pieces.append(weight.astype(jnp.bfloat16))
        top[...] = high
        total[...] = summed
        acc[...] = acc[...] * fade + jnp.dot(
            jnp.concatenate(pieces, axis=1),
            pairs[chunk % 2, 1],
            preferred_element_type=jnp.float32,
        )

    arrive(0)

    @pl.when(left > 0)
    def _():
        score(0)

    for chunk in range(CHUNKS):
        if chunk + 1 < CHUNKS:
            arrive(chunk + 1)

        @pl.when(chunk * CHUNK_SOURCES * 2 * PIECE < left)
        def _(chunk=chunk):
            if chunk + 1 < CHUNKS:
                score(chunk + 1)
            fold(chunk)

    count = jnp.sum(total[...], axis=1, keepdims=True)
    some = count > 0.0
    safe = jnp.where(some, count, 1.0)
    out_ref[pl.ds(0, HEAD_ROWS), :] = (acc[...] / safe).astype(jnp.bfloat16)
    level = jnp.where(some, top[...] + jnp.log(safe), NEGATIVE)
    level = jnp.sum(jnp.where(row == lane, level, 0.0), axis=0, keepdims=True)
    first = level.astype(jnp.bfloat16).astype(jnp.float32)
    second = (level - first).astype(jnp.bfloat16).astype(jnp.float32)
    third = level - first - second
    place_in = lax.broadcasted_iota(jnp.int32, (16, HD), 0)
    parts = jnp.where(place_in == 0, first, jnp.where(place_in == 1, second, third))
    out_ref[pl.ds(HEAD_ROWS, 16), :] = parts.astype(jnp.bfloat16)

    for index in range(CTX // GROUP):
        place(index).wait()


def attend(info, moved, sums, cosine, sine):
    anywhere = pl.BlockSpec(memory_space=pl.ANY)
    vmem = pl.BlockSpec(memory_space=pltpu.VMEM)
    return pl.pallas_call(
        attend_kernel,
        in_specs=[pl.BlockSpec(memory_space=pltpu.SMEM), anywhere] + [vmem] * 6,
        out_specs=[anywhere, vmem],
        scratch_shapes=[
            pltpu.VMEM((CTX, TP, 2 * PIECE, HD), jnp.bfloat16),
            pltpu.VMEM((CHUNK_ROWS, HD), jnp.float32),
            pltpu.VMEM((2, 2, CHUNK_KEYS, HD), jnp.bfloat16),
            pltpu.VMEM((HEAD_ROWS, HD), jnp.bfloat16),
            pltpu.VMEM((2, HEAD_ROWS, CHUNK_KEYS), jnp.float32),
            pltpu.VMEM((2, HEAD_ROWS, HD), jnp.float32),
            pltpu.VMEM((HEAD_ROWS, HD), jnp.float32),
            pltpu.VMEM((HEAD_ROWS, HD), jnp.float32),
            pltpu.VMEM((HEAD_ROWS, HD), jnp.float32),
            pltpu.SemaphoreType.DMA((CTX // GROUP,)),
            pltpu.SemaphoreType.DMA((CTX // GROUP,)),
        ],
        out_shape=[
            jax.ShapeDtypeStruct((CTX, TP, 2 * PIECE, HD), jnp.bfloat16),
            jax.ShapeDtypeStruct((STATE_ROWS, HD), jnp.bfloat16),
        ],
        compiler_params=pltpu.CompilerParams(vmem_limit_bytes=32 * 1024 * 1024),
        name="attend",
    )(info, moved, *sums, cosine, sine)


def project_kernel(states_ref, w_ref, *refs):
    base_ref, out_ref = refs if len(refs) == 2 else (None, refs[0])
    row = lax.broadcasted_iota(jnp.int32, (HEAD_ROWS, HD), 0)
    lane = lax.broadcasted_iota(jnp.int32, (HEAD_ROWS, HD), 1)
    many = REQUESTS * HEAD_ROWS
    target = lax.broadcasted_iota(jnp.int32, (many, many), 0)
    origin = lax.broadcasted_iota(jnp.int32, (many, many), 1)
    head = target // (STEPS * REQUESTS)
    step = target // REQUESTS % STEPS
    request = target % REQUESTS
    moves = jnp.where(origin == request * HEAD_ROWS + head * STEPS + step, 1.0, 0.0)
    rows = []
    for request in range(REQUESTS):
        spots = [2 * request + part for part in range(2)]
        levels = []
        for spot in spots:
            coded = states_ref[spot, pl.ds(HEAD_ROWS, 16), :].astype(jnp.float32)
            level = coded[0:1] + coded[1:2] + coded[2:3]
            levels.append(jnp.sum(jnp.where(row == lane, level, 0.0), axis=1, keepdims=True))
        high = jnp.maximum(levels[0], levels[1])
        shares = [jnp.exp(level - high) for level in levels]
        whole = shares[0] + shares[1]
        mixed = sum(
            states_ref[spot, pl.ds(0, HEAD_ROWS), :].astype(jnp.float32) * (share / whole)
            for spot, share in zip(spots, shares)
        )
        rows.append(mixed.astype(jnp.bfloat16))
    attn = jnp.dot(
        moves.astype(jnp.bfloat16),
        jnp.concatenate(rows, axis=0),
        preferred_element_type=jnp.float32,
    ).astype(jnp.bfloat16)
    total = jnp.zeros(out_ref.shape, jnp.float32)
    for index in range(GQA):
        total = total + jnp.dot(
            attn[index * HEAD_ROWS:(index + 1) * HEAD_ROWS],
            w_ref[pl.ds(index * HD, HD), :],
            preferred_element_type=jnp.float32,
        )
    if base_ref is not None:
        total = total + base_ref[...]
    out_ref[...] = total.astype(out_ref.dtype)


def project(states, w, base=None):
    vmem = pl.BlockSpec(memory_space=pltpu.VMEM)
    operands = (states, w) if base is None else (states, w, base)
    kind = jnp.float32 if base is None else jnp.bfloat16
    return pl.pallas_call(
        project_kernel,
        in_specs=[vmem] * len(operands),
        out_specs=vmem,
        out_shape=jax.ShapeDtypeStruct((STEPS * REQUESTS, w.shape[1]), kind),
        compiler_params=pltpu.CompilerParams(vmem_limit_bytes=8 * 1024 * 1024),
        name="project",
    )(*operands)


def per_device(hidden_states, norm_gain, prompt_lengths, kv_cache, w_qkv, w_out):
    x = lax.axis_index("x")
    y = lax.axis_index("y")
    mine = x * (REQUESTS // SIDE) + y // 2
    part = y % 2
    length = lax.dynamic_index_in_dim(prompt_lengths, mine, 0, keepdims=False)

    ready = prep(kv_cache).reshape(CTX * TP, 2 * PIECE, HD)
    everyone = ("x", "y", "z", "core")
    moved = lax.all_to_all(ready, everyone, split_axis=0, concat_axis=0, tiled=True)
    moved = moved.reshape(CTX, TP, 2 * PIECE, HD)

    _, hidden_states = lax.optimization_barrier((ready, hidden_states))
    packed = partial_projection(x, hidden_states, norm_gain, w_qkv)
    packed, w_out = lax.optimization_barrier((packed, w_out))
    along_x = packed[0] + sum(swap(packed[k], "x", k) for k in range(1, SIDE))
    w_mate = swap(w_out, "core", 1)
    along_x = along_x.reshape(2, STEPS, COLUMNS + HD)
    own = lax.dynamic_index_in_dim(along_x, y // 2, 0, keepdims=False)
    far = lax.dynamic_index_in_dim(along_x, 1 - y // 2, 0, keepdims=False)
    sums = [own, swap(own, "y", 1), swap(far, "y", 3), swap(far, "y", 2)]

    angle = angles(length + jnp.arange(STEPS, dtype=jnp.int32), HD)
    cosine = jnp.cos(angle)
    sine = jnp.sin(angle)
    cosine = jnp.concatenate([cosine, cosine], axis=1)
    sine = jnp.concatenate([-sine, sine], axis=1)
    info = jnp.stack([length, part]).astype(jnp.int32)
    kv_decode, state = attend(info, moved, sums, cosine, sine)
    kv_decode = kv_decode.reshape(1, SOURCES, PIECE, 2, HD)

    states = jnp.broadcast_to(state[None], (CTX, STATE_ROWS, HD))
    states = lax.all_to_all(states, ("x", "y"), split_axis=0, concat_axis=0, tiled=True)
    mate_states = swap(states, "core", 1)
    out = project(mate_states, w_mate, project(states, w_out))
    pairs = [(z * 2 + c, (z ^ (1 + 2 * c)) * 2 + c) for z in range(SIDE) for c in range(2)]
    near = lax.ppermute(out, ("z", "core"), pairs)
    across = swap(out, "z", 2)
    shared = swap(near, "core", 1)
    first = lax.axis_index("core") == 0
    one = jnp.where(first, near, shared).astype(jnp.float32)
    three = jnp.where(first, shared, near).astype(jnp.float32)
    block_out = (out.astype(jnp.float32) + one) + (across.astype(jnp.float32) + three)
    block_out = block_out.astype(jnp.bfloat16)
    return (block_out, kv_decode)


def solution(mesh):
    fine = jax.sharding.Mesh(
        mesh.devices.reshape(SIDE, SIDE, SIDE, 2), ("x", "y", "z", "core")
    )
    ctx, tp = ("x", "y"), ("z", "core")
    return jax.shard_map(
        per_device,
        mesh=fine,
        in_specs=(
            P(None, ctx),
            P(ctx),
            P(),
            P(None, ctx + tp, None, None),
            P(ctx, tp),
            P(tp, ctx),
        ),
        out_specs=(P(None, ctx), P(ctx, None, None, None, tp)),
        check_vma=False,
    )
```

```python
import math

import jax
import jax.numpy as jnp
from jax import lax
from jax.experimental import pallas as pl
from jax.experimental.pallas import tpu as pltpu
from jax.sharding import PartitionSpec as P

D = 8192
HD = 128
STEPS = 4
GQA = 8
REQUESTS = 8
SOURCES = 128
PIECE = 64
TP = 8
CTX = 16
HEAD_ROWS = STEPS * GQA

ROPE_BASE = 500000.0
ROPE_FACTOR = 8.0
LOW_FACTOR = 1.0
HIGH_FACTOR = 4.0
ROPE_ANCHOR = 8192.0
NEGATIVE = -1e30
SCALE = HD ** (-0.5)


def angles(positions, width):
    base_freq = ROPE_BASE ** (-(2.0 * jnp.arange(width // 2, dtype=jnp.float32)) / width)
    wavelength = 2.0 * math.pi / base_freq
    blend = (ROPE_ANCHOR / wavelength - LOW_FACTOR) / (HIGH_FACTOR - LOW_FACTOR)
    middle = (1.0 - blend) * base_freq / ROPE_FACTOR + blend * base_freq
    freq = jnp.where(
        wavelength > ROPE_ANCHOR / LOW_FACTOR,
        base_freq / ROPE_FACTOR,
        jnp.where(wavelength < ROPE_ANCHOR / HIGH_FACTOR, base_freq, middle),
    )
    return positions.astype(jnp.float32)[..., None] * freq


COLUMNS = (GQA + 2) * HD
SIDE = 4


def partial_kernel(x_ref, hidden_ref, gain_ref, w_ref, *out_refs):
    rows = STEPS * REQUESTS
    share = rows // SIDE
    target = lax.broadcasted_iota(jnp.int32, (rows, rows), 0)
    origin = lax.broadcasted_iota(jnp.int32, (rows, rows), 1)
    receiver = jnp.bitwise_xor(target // share, x_ref[0])
    request = receiver * (REQUESTS // SIDE) + target % share // STEPS
    moves = jnp.where(origin == target % STEPS * REQUESTS + request, 1.0, 0.0)
    values = jnp.dot(
        moves.astype(jnp.bfloat16), hidden_ref[...], preferred_element_type=jnp.float32
    )
    square = jnp.sum(values * values, axis=1, keepdims=True)
    gain = gain_ref[...].astype(jnp.float32).reshape(1, -1)
    scaled = (values * gain).astype(jnp.bfloat16)
    proj = jnp.dot(scaled, w_ref[...], preferred_element_type=jnp.float32)
    square = jnp.broadcast_to(square, (rows, HD))
    for index, out_ref in enumerate(out_refs):
        out_ref[:, pl.ds(0, COLUMNS)] = proj[index * share:(index + 1) * share]
        out_ref[:, pl.ds(COLUMNS, HD)] = square[index * share:(index + 1) * share]


def partial_projection(x, hidden_states, norm_gain, w_qkv):
    vmem = pl.BlockSpec(memory_space=pltpu.VMEM)
    shape = jax.ShapeDtypeStruct((STEPS * REQUESTS // SIDE, COLUMNS + HD), jnp.float32)
    return pl.pallas_call(
        partial_kernel,
        in_specs=[pl.BlockSpec(memory_space=pltpu.SMEM), vmem, vmem, vmem],
        out_specs=[vmem] * SIDE,
        out_shape=[shape] * SIDE,
        compiler_params=pltpu.CompilerParams(vmem_limit_bytes=8 * 1024 * 1024),
        name="partial_projection",
    )(x.reshape(1), hidden_states, norm_gain, w_qkv)


def swap(value, axis, other):
    pairs = [(index, index ^ other) for index in range(lax.axis_size(axis))]
    return lax.ppermute(value, axis, pairs)


GROUP = 2


def prep_kernel(kv_ref, out_ref, held, ready, in_sems, out_sems):
    def fetch(index):
        span = pl.ds(index * GROUP, GROUP)
        return pltpu.make_async_copy(kv_ref.at[span], held.at[span], in_sems.at[index])

    def place(index):
        span = pl.ds(index * GROUP, GROUP)
        return pltpu.make_async_copy(ready.at[span], out_ref.at[span], out_sems.at[index])

    for index in range(CTX // GROUP):
        fetch(index).start()
    for index in range(CTX // GROUP):
        fetch(index).wait()
        for receiver in range(index * GROUP, (index + 1) * GROUP):
            for head in range(TP):
                ready[receiver, head] = held[receiver, :, :, pl.ds(head * HD, HD)]
        place(index).start()
    for index in range(CTX // GROUP):
        place(index).wait()


def prep(kv_cache):
    split = kv_cache.reshape(CTX, PIECE, 2, TP * HD)
    return pl.pallas_call(
        prep_kernel,
        out_shape=jax.ShapeDtypeStruct((CTX, TP, PIECE, 2, HD), jnp.bfloat16),
        in_specs=[pl.BlockSpec(memory_space=pl.ANY)],
        out_specs=pl.BlockSpec(memory_space=pl.ANY),
        scratch_shapes=[
            pltpu.VMEM((CTX, PIECE, 2, TP * HD), jnp.bfloat16),
            pltpu.VMEM((CTX, TP, PIECE, 2, HD), jnp.bfloat16),
            pltpu.SemaphoreType.DMA((CTX // GROUP,)),
            pltpu.SemaphoreType.DMA((CTX // GROUP,)),
        ],
        compiler_params=pltpu.CompilerParams(vmem_limit_bytes=56 * 1024 * 1024),
        cost_estimate=pl.CostEstimate(
            flops=0, transcendentals=0, bytes_accessed=4 * kv_cache.size
        ),
        name="cache_by_receiver",
    )(split)


CHUNKS = 4
CHUNK_CTX = CTX // CHUNKS
CHUNK_SOURCES = SOURCES // CHUNKS
CHUNK_KEYS = CHUNK_SOURCES * PIECE
CHUNK_ROWS = CHUNK_KEYS * 2
STATE_ROWS = HEAD_ROWS + 16


def attend_kernel(
    info_ref, kv_ref, own_ref, first_ref, second_ref, third_ref, cos_ref, sin_ref,
    kv_out_ref, out_ref,
    held, wide, pairs, query, scores, peaks, top, total, acc, in_sems, out_sems,
):
    length = info_ref[0]
    part = info_ref[1]
    left = length - part * PIECE

    def fetch(index):
        span = pl.ds(index * GROUP, GROUP)
        return pltpu.make_async_copy(kv_ref.at[span], held.at[span], in_sems.at[index])

    def place(index):
        span = pl.ds(index * GROUP, GROUP)
        return pltpu.make_async_copy(held.at[span], kv_out_ref.at[span], out_sems.at[index])

    for index in range(CTX // GROUP):
        fetch(index).start()

    row = lax.broadcasted_iota(jnp.int32, (HEAD_ROWS, HD), 0)
    lane = lax.broadcasted_iota(jnp.int32, (HEAD_ROWS, HD), 1)
    slot = lane // PIECE * (2 * PIECE) + lane % PIECE

    summed = own_ref[...] + first_ref[...] + second_ref[...] + third_ref[...]
    norm = lax.rsqrt(summed[:, COLUMNS:] / D + 1e-05)

    def head(index):
        return summed[:, index * HD:(index + 1) * HD] * norm

    def turn(vec):
        return vec * cos_ref[...] + pltpu.roll(vec, HD // 2, 1) * sin_ref[...]

    query[...] = jnp.concatenate([turn(head(g)) for g in range(GQA)], axis=0).astype(jnp.bfloat16)
    rest = jnp.zeros((HD - STEPS, HD), jnp.float32)
    keys = jnp.concatenate([turn(head(GQA)), rest], axis=0).astype(jnp.bfloat16)
    values = jnp.concatenate([head(GQA + 1), rest], axis=0).astype(jnp.bfloat16)
    fresh = lax.dot_general(
        query[...], keys, (((1,), (1,)), ((), ())), preferred_element_type=jnp.float32
    ) * SCALE
    live = jnp.logical_and(lane <= row % STEPS, part == 0)
    fresh = jnp.where(live, fresh, NEGATIVE)
    high = jnp.max(fresh, axis=1, keepdims=True)
    weight = jnp.where(live, jnp.exp(fresh - high), 0.0)
    top[...] = jnp.broadcast_to(high, (HEAD_ROWS, HD))
    total[...] = weight
    acc[...] = jnp.dot(weight.astype(jnp.bfloat16), values, preferred_element_type=jnp.float32)

    def arrive(chunk):
        for index in range(chunk * CHUNK_CTX // GROUP, (chunk + 1) * CHUNK_CTX // GROUP):
            fetch(index).wait()
            place(index).start()

    def score(chunk):
        wide[...] = held[pl.ds(chunk * CHUNK_CTX, CHUNK_CTX)].reshape(CHUNK_ROWS, HD).astype(
            jnp.float32
        )
        for index in range(2):
            pairs[chunk % 2, index] = wide[pl.ds(index, CHUNK_KEYS, stride=2), :].astype(
                jnp.bfloat16
            )
        found = lax.dot_general(
            query[...],
            pairs[chunk % 2, 0],
            (((1,), (1,)), ((), ())),
            preferred_element_type=jnp.float32,
        )
        peak = None
        for index in range(CHUNK_KEYS // HD):
            source = chunk * CHUNK_SOURCES + index * 2
            piece = found[:, index * HD:(index + 1) * HD] * SCALE
            piece = jnp.where(slot < left - source * (2 * PIECE), piece, NEGATIVE)
            scores[chunk % 2, :, pl.ds(index * HD, HD)] = piece
            peak = piece if peak is None else jnp.maximum(peak, piece)
        peaks[chunk % 2] = peak

    def fold(chunk):
        high = jnp.maximum(top[...], jnp.max(peaks[chunk % 2], axis=1, keepdims=True))
        fade = jnp.exp(top[...] - high)
        summed = total[...] * fade
        pieces = []
        for index in range(CHUNK_KEYS // HD):
            weight = jnp.exp(scores[chunk % 2, :, pl.ds(index * HD, HD)] - high)
            summed = summed + weight
            pieces.append(weight.astype(jnp.bfloat16))
        top[...] = high
        total[...] = summed
        acc[...] = acc[...] * fade + jnp.dot(
            jnp.concatenate(pieces, axis=1),
            pairs[chunk % 2, 1],
            preferred_element_type=jnp.float32,
        )

    arrive(0)

    @pl.when(left > 0)
    def _():
        score(0)

    for chunk in range(CHUNKS):
        if chunk + 1 < CHUNKS:
            arrive(chunk + 1)

        @pl.when(chunk * CHUNK_SOURCES * 2 * PIECE < left)
        def _(chunk=chunk):
            if chunk + 1 < CHUNKS:
                score(chunk + 1)
            fold(chunk)

    count = jnp.sum(total[...], axis=1, keepdims=True)
    some = count > 0.0
    safe = jnp.where(some, count, 1.0)
    out_ref[pl.ds(0, HEAD_ROWS), :] = (acc[...] / safe).astype(jnp.bfloat16)
    level = jnp.where(some, top[...] + jnp.log(safe), NEGATIVE)
    level = jnp.sum(jnp.where(row == lane, level, 0.0), axis=0, keepdims=True)
    first = level.astype(jnp.bfloat16).astype(jnp.float32)
    second = (level - first).astype(jnp.bfloat16).astype(jnp.float32)
    third = level - first - second
    place_in = lax.broadcasted_iota(jnp.int32, (16, HD), 0)
    parts = jnp.where(place_in == 0, first, jnp.where(place_in == 1, second, third))
    out_ref[pl.ds(HEAD_ROWS, 16), :] = parts.astype(jnp.bfloat16)

    for index in range(CTX // GROUP):
        place(index).wait()


def attend(info, moved, sums, cosine, sine):
    anywhere = pl.BlockSpec(memory_space=pl.ANY)
    vmem = pl.BlockSpec(memory_space=pltpu.VMEM)
    return pl.pallas_call(
        attend_kernel,
        in_specs=[pl.BlockSpec(memory_space=pltpu.SMEM), anywhere] + [vmem] * 6,
        out_specs=[anywhere, vmem],
        scratch_shapes=[
            pltpu.VMEM((CTX, TP, 2 * PIECE, HD), jnp.bfloat16),
            pltpu.VMEM((CHUNK_ROWS, HD), jnp.float32),
            pltpu.VMEM((2, 2, CHUNK_KEYS, HD), jnp.bfloat16),
            pltpu.VMEM((HEAD_ROWS, HD), jnp.bfloat16),
            pltpu.VMEM((2, HEAD_ROWS, CHUNK_KEYS), jnp.float32),
            pltpu.VMEM((2, HEAD_ROWS, HD), jnp.float32),
            pltpu.VMEM((HEAD_ROWS, HD), jnp.float32),
            pltpu.VMEM((HEAD_ROWS, HD), jnp.float32),
            pltpu.VMEM((HEAD_ROWS, HD), jnp.float32),
            pltpu.SemaphoreType.DMA((CTX // GROUP,)),
            pltpu.SemaphoreType.DMA((CTX // GROUP,)),
        ],
        out_shape=[
            jax.ShapeDtypeStruct((CTX, TP, 2 * PIECE, HD), jnp.bfloat16),
            jax.ShapeDtypeStruct((STATE_ROWS, HD), jnp.bfloat16),
        ],
        compiler_params=pltpu.CompilerParams(vmem_limit_bytes=24 * 1024 * 1024),
        name="attend",
    )(info, moved, *sums, cosine, sine)


def combine_kernel(states_ref, out_ref):
    row = lax.broadcasted_iota(jnp.int32, (HEAD_ROWS, HD), 0)
    lane = lax.broadcasted_iota(jnp.int32, (HEAD_ROWS, HD), 1)
    many = REQUESTS * HEAD_ROWS
    target = lax.broadcasted_iota(jnp.int32, (many, many), 0)
    origin = lax.broadcasted_iota(jnp.int32, (many, many), 1)
    head = target // (STEPS * REQUESTS)
    step = target // REQUESTS % STEPS
    request = target % REQUESTS
    moves = jnp.where(origin == request * HEAD_ROWS + head * STEPS + step, 1.0, 0.0)
    rows = []
    for request in range(REQUESTS):
        spots = [2 * request + part for part in range(2)]
        levels = []
        for spot in spots:
            coded = states_ref[spot, pl.ds(HEAD_ROWS, 16), :].astype(jnp.float32)
            level = coded[0:1] + coded[1:2] + coded[2:3]
            levels.append(jnp.sum(jnp.where(row == lane, level, 0.0), axis=1, keepdims=True))
        high = jnp.maximum(levels[0], levels[1])
        shares = [jnp.exp(level - high) for level in levels]
        whole = shares[0] + shares[1]
        mixed = sum(
            states_ref[spot, pl.ds(0, HEAD_ROWS), :].astype(jnp.float32) * (share / whole)
            for spot, share in zip(spots, shares)
        )
        rows.append(mixed.astype(jnp.bfloat16))
    out_ref[...] = jnp.dot(
        moves.astype(jnp.bfloat16),
        jnp.concatenate(rows, axis=0),
        preferred_element_type=jnp.float32,
    ).astype(jnp.bfloat16)


def combine(states):
    vmem = pl.BlockSpec(memory_space=pltpu.VMEM)
    return pl.pallas_call(
        combine_kernel,
        in_specs=[vmem],
        out_specs=vmem,
        out_shape=jax.ShapeDtypeStruct((REQUESTS * HEAD_ROWS, HD), jnp.bfloat16),
        compiler_params=pltpu.CompilerParams(vmem_limit_bytes=8 * 1024 * 1024),
        name="combine",
    )(states)


def project_kernel(attn_ref, w_ref, *refs):
    base_ref, out_ref = refs if len(refs) == 2 else (None, refs[0])
    total = jnp.zeros(out_ref.shape, jnp.float32)
    for index in range(GQA):
        total = total + jnp.dot(
            attn_ref[pl.ds(index * HEAD_ROWS, HEAD_ROWS), :],
            w_ref[pl.ds(index * HD, HD), :],
            preferred_element_type=jnp.float32,
        )
    if base_ref is not None:
        total = total + base_ref[...]
    out_ref[...] = total.astype(out_ref.dtype)


def project(attn, w, base=None):
    vmem = pl.BlockSpec(memory_space=pltpu.VMEM)
    operands = (attn, w) if base is None else (attn, w, base)
    kind = jnp.float32 if base is None else jnp.bfloat16
    return pl.pallas_call(
        project_kernel,
        in_specs=[vmem] * len(operands),
        out_specs=vmem,
        out_shape=jax.ShapeDtypeStruct((STEPS * REQUESTS, w.shape[1]), kind),
        compiler_params=pltpu.CompilerParams(vmem_limit_bytes=8 * 1024 * 1024),
        name="project",
    )(*operands)


def per_device(hidden_states, norm_gain, prompt_lengths, kv_cache, w_qkv, w_out):
    x = lax.axis_index("x")
    y = lax.axis_index("y")
    mine = x * (REQUESTS // SIDE) + y // 2
    part = y % 2
    length = lax.dynamic_index_in_dim(prompt_lengths, mine, 0, keepdims=False)

    ready = prep(kv_cache).reshape(CTX * TP, 2 * PIECE, HD)
    everyone = ("x", "y", "z", "core")
    moved = lax.all_to_all(ready, everyone, split_axis=0, concat_axis=0, tiled=True)
    moved = moved.reshape(CTX, TP, 2 * PIECE, HD)

    _, hidden_states = lax.optimization_barrier((ready, hidden_states))
    packed = partial_projection(x, hidden_states, norm_gain, w_qkv)
    packed, w_out = lax.optimization_barrier((packed, w_out))
    along_x = packed[0] + sum(swap(packed[k], "x", k) for k in range(1, SIDE))
    w_mate = swap(w_out, "core", 1)
    along_x = along_x.reshape(2, STEPS, COLUMNS + HD)
    own = lax.dynamic_index_in_dim(along_x, y // 2, 0, keepdims=False)
    far = lax.dynamic_index_in_dim(along_x, 1 - y // 2, 0, keepdims=False)
    sums = [own, swap(own, "y", 1), swap(far, "y", 3), swap(far, "y", 2)]

    angle = angles(length + jnp.arange(STEPS, dtype=jnp.int32), HD)
    cosine = jnp.cos(angle)
    sine = jnp.sin(angle)
    cosine = jnp.concatenate([cosine, cosine], axis=1)
    sine = jnp.concatenate([-sine, sine], axis=1)
    info = jnp.stack([length, part]).astype(jnp.int32)
    kv_decode, state = attend(info, moved, sums, cosine, sine)
    kv_decode = kv_decode.reshape(1, SOURCES, PIECE, 2, HD)

    states = jnp.broadcast_to(state[None], (CTX, STATE_ROWS, HD))
    states = lax.all_to_all(states, ("x", "y"), split_axis=0, concat_axis=0, tiled=True)
    attn = combine(states)
    mate_attn = swap(attn, "core", 1)
    out = project(mate_attn, w_mate, project(attn, w_out))
    pairs = [(z * 2 + c, (z ^ (1 + 2 * c)) * 2 + c) for z in range(SIDE) for c in range(2)]
    near = lax.ppermute(out, ("z", "core"), pairs)
    across = swap(out, "z", 2)
    shared = swap(near, "core", 1)
    first = lax.axis_index("core") == 0
    one = jnp.where(first, near, shared).astype(jnp.float32)
    three = jnp.where(first, shared, near).astype(jnp.float32)
    block_out = (out.astype(jnp.float32) + one) + (across.astype(jnp.float32) + three)
    block_out = block_out.astype(jnp.bfloat16)
    return (block_out, kv_decode)


def solution(mesh):
    fine = jax.sharding.Mesh(
        mesh.devices.reshape(SIDE, SIDE, SIDE, 2), ("x", "y", "z", "core")
    )
    ctx, tp = ("x", "y"), ("z", "core")
    return jax.shard_map(
        per_device,
        mesh=fine,
        in_specs=(
            P(None, ctx),
            P(ctx),
            P(),
            P(None, ctx + tp, None, None),
            P(ctx, tp),
            P(tp, ctx),
        ),
        out_specs=(P(None, ctx), P(ctx, None, None, None, tp)),
        check_vma=False,
    )
```
